32 devices in a mesh: hst: 8 (over z, y), dev: 4 (over x, core).
Axes of the slice: x: 2, y: 2, z: 4, core: 2. Of those that a mesh axis runs over, the one named last changes fastest.
Arguments:
- weight_rows: float32 [8704, 3072], P(('hst', 'dev')), may hold values from -1.5 to 1.5
- moment_rows: float32 [8704, 3072], P(('hst', 'dev')), may hold values from -6 to 6
- grad_rows: bfloat16 [9376, 3072], P(('hst', 'dev')), may hold values from -6 to 6
- basis: float32 [3072, 256], P(('hst', 'dev')), may hold values from -6 to 6
- old_bounds: int32 [33], replicated, may hold values from 0 to 8192, as said below
- new_bounds: int32 [33], replicated, may hold values from 0 to 8192, as said below
Outputs:
- weight_out: float32 [9376, 3072], P(('hst', 'dev'))
- moment_out: float32 [9376, 3072], P(('hst', 'dev'))
- right_basis_result: float32 [3072, 256], replicated
The draws below stay inside these ranges and needn't reach their ends.
Inputs may be any that keep to these rules, and one draw needn't show every extreme that they name: old_bounds[i] is i * (256) plus an offset of 0 to 16, the first 0 and the last 8192; some device owns exactly 272 rows. `new_bounds`: the devices of one host, neither the first nor the last, own no rows; the others, counted s = 0 to 27 in mesh order, own rows floor(s * 8192 / 28) to floor((s + 1) * 8192 / 28) - 1, so some own exactly 293 rows.
All inputs are finite; a program needn't handle non-finite values.
Results may differ from the reference program's by a relative error of at most 0.0003.
Values may be sent and summed in bfloat16 or wider, within the bound.
No kernel may reach another device: no remote copies, remote signals or barrier semaphores. Data moves between devices by JAX's collectives and lax.ppermute only.
A program may use at most 192 MiB of HBM per device.

```python
import math
import jax
import jax.numpy as jnp
from jax import lax

HIDDEN_ROWS = 8192
COLS = 3072
RANK = 256
JIT = 16
OLD_CAP = 272
NEW_CAP = 293
N_HST = 8
N_DEV = 4
DEVICES = 32


def draw_old_bounds(key, part):
    key = jax.random.fold_in(key, 11)
    jitter_key, peak_key = jax.random.split(key)
    average = HIDDEN_ROWS // DEVICES
    jitter = jax.random.randint(jitter_key, (DEVICES + 1,), 0, JIT + 1)
    peak_slot = jax.random.randint(peak_key, (), 0, DEVICES - 1)
    jitter = jitter.at[peak_slot].set(0).at[peak_slot + 1].set(JIT)
    jitter = jitter.at[0].set(0).at[DEVICES].set(0)
    return (jnp.arange(DEVICES + 1, dtype=jnp.int32) * average + jitter).astype(jnp.int32)


def draw_new_bounds(key, part):
    key = jax.random.fold_in(key, 23)
    lost_host = jax.random.randint(key, (), 1, N_HST - 1)
    remaining_hosts = DEVICES - N_DEV
    flat_ids = jnp.arange(DEVICES + 1, dtype=jnp.int32)
    lost_start = lost_host * N_DEV
    rank_numbers = jnp.where(flat_ids <= lost_start, flat_ids, jnp.maximum(flat_ids - N_DEV, lost_start))
    return (rank_numbers * HIDDEN_ROWS // remaining_hosts).astype(jnp.int32)


def steps_of(stream_key, shape, cuts, low, top_value):
    factor_of = 1.0
    for dim, blocks in cuts:
        steps = jax.random.uniform(jax.random.fold_in(jax.random.fold_in(stream_key, 6), dim), (blocks,), jnp.float32, low / len(cuts), top_value / len(cuts))
        factor_of = factor_of * jnp.repeat(jnp.exp(steps), shape[dim] // blocks).reshape((-1,) + (1,) * (len(shape) - 1 - dim))
    return factor_of


def bell_draw(rng, extent, deviation, bound, pieces=(), held_as=jnp.bfloat16):
    values = deviation * jax.random.normal(rng, extent, jnp.float32)
    if pieces:
        values = values * steps_of(rng, extent, pieces, -0.22, 0.18)
    return jnp.clip(values, -bound, bound).astype(held_as)


def setup_inputs(seed: int = 0) -> dict:
    splits = jax.random.split(jax.random.key(seed), 7)
    return {
        "weight_rows": bell_draw(splits[0], (DEVICES * OLD_CAP, COLS), 0.25, 1.5, ((0, 32),), jnp.float32),
        "moment_rows": bell_draw(splits[1], (DEVICES * OLD_CAP, COLS), 1.0, 6.0, ((0, 32),), jnp.float32),
        "grad_rows": bell_draw(splits[2], (DEVICES * NEW_CAP, COLS), 1.0, 6.0, ((0, 32),)),
        "basis": bell_draw(splits[3], (COLS, RANK), 1.0, 6.0, ((0, 32),), jnp.float32),
        "old_bounds": draw_old_bounds(jax.random.fold_in(splits[6], 71), 0),
        "new_bounds": draw_new_bounds(jax.random.fold_in(splits[6], 71), 0),
    }


def rows_from_slots(slot_rows, bounds, capacity):
    row_ids = jnp.arange(HIDDEN_ROWS, dtype=jnp.int32)
    owner_index = (jnp.searchsorted(bounds, row_ids, side='right') - 1).astype(jnp.int32)
    position = owner_index * capacity + row_ids - bounds[owner_index].astype(jnp.int32)
    return slot_rows[position]

def reference(weight_rows, moment_rows, grad_rows, basis, old_bounds, new_bounds):
    highest = lax.Precision.HIGHEST
    weight = rows_from_slots(weight_rows, old_bounds, OLD_CAP)
    moment_buffer = rows_from_slots(moment_rows, old_bounds, OLD_CAP)
    gradient_matrix = rows_from_slots(grad_rows, new_bounds, NEW_CAP)
    mixed = moment_buffer + gradient_matrix.astype(jnp.float32)
    projected = jnp.dot(mixed.astype(jnp.float32), basis.astype(jnp.float32), precision=highest, preferred_element_type=jnp.float32)
    gram_matrix = jnp.dot(projected.T.astype(jnp.float32), projected.astype(jnp.float32), precision=highest, preferred_element_type=jnp.float32)
    factor = jnp.linalg.cholesky(gram_matrix)
    orthonormal = lax.linalg.triangular_solve(factor, projected, left_side=False, lower=True, transpose_a=True)
    reduced = jnp.dot(mixed.T.astype(jnp.float32), orthonormal.astype(jnp.float32), precision=highest, preferred_element_type=jnp.float32)
    moment_new = mixed - (1.0 - 0.6) * jnp.dot(orthonormal.astype(jnp.float32), reduced.T.astype(jnp.float32), precision=highest, preferred_element_type=jnp.float32)
    column_rms = jnp.sqrt(lax.optimization_barrier(jnp.mean(reduced * reduced, axis=0)) + 1e-06)
    right_basis_result = reduced / column_rms[None, :]
    update = jnp.dot(orthonormal.astype(jnp.float32), right_basis_result.T.astype(jnp.float32), precision=highest, preferred_element_type=jnp.float32)
    weight_new = (1.0 - 0.1 * 0.5) * weight - 0.1 * 0.2 * math.sqrt(HIDDEN_ROWS / RANK) * update
    slot_ids = jnp.arange(DEVICES * NEW_CAP, dtype=jnp.int32)
    device_ids = slot_ids // NEW_CAP
    wanted = new_bounds[device_ids].astype(jnp.int32) + slot_ids - device_ids * NEW_CAP
    is_live = wanted < new_bounds[device_ids + 1].astype(jnp.int32)
    wanted = jnp.where(is_live, wanted, 0)
    weight_out = jnp.where(is_live[:, None], weight_new[wanted], jnp.float32(0.0))
    moment_out = jnp.where(is_live[:, None], moment_new[wanted], jnp.float32(0.0))
    return (weight_out, moment_out, right_basis_result)
```

```python
import math

import jax
import jax.numpy as jnp
import numpy as np
from jax import lax
from jax.sharding import PartitionSpec as P

HIDDEN_ROWS = 8192
RANK = 256
AXES = ("hst", "dev")
HIGHEST = lax.Precision.HIGHEST

momentum_rate = 0.6
learn_rate = 0.1
decay_rate = 0.5
update_rms = 0.2
epsilon = 1e-06

BLOCK = 64
WIRE = jnp.float16
WEIGHT_SCALE = 2.0**15
MOMENT_SCALE = 2.0**13


def new_ranges(lost, hosts, per_host):
    left = (hosts - 1) * per_host
    ids = np.arange(hosts * per_host + 1)
    first = lost * per_host
    rank = np.where(ids <= first, ids, np.maximum(ids - per_host, first))
    return rank * HIDDEN_ROWS // left


def plan_blocks(bounds, old_cap, new_cap):
    count = len(bounds) - 1
    even = HIDDEN_ROWS // count
    blocks = []
    for start in range(0, new_cap, BLOCK):
        edges = []
        for dst in range(count):
            low = bounds[dst] + start
            high = min(low + BLOCK, bounds[dst + 1])
            if low >= high:
                continue
            for src in range(count):
                src_low = src * even
                src_high = min(src * even + old_cap, HIDDEN_ROWS)
                size = min(high, src_high) - max(low, src_low)
                if size > 0:
                    edges.append((-size, src, dst))
        edges.sort()
        rounds = []
        for _, src, dst in edges:
            for pairs in rounds:
                if all(src != a and dst != b for a, b in pairs):
                    pairs.append((src, dst))
                    break
            else:
                rounds.append([(src, dst)])
        blocks.append((start, rounds))
    return blocks


def flip(value, count, bit):
    return lax.ppermute(value, AXES, [(i, i ^ (1 << bit)) for i in range(count)])


def gather_bits(value, me, count, order):
    held = []
    for bit in order:
        other = flip(value, count, bit)
        axis = sum(b > bit for b in held)
        mine = (me >> bit) & 1
        value = jnp.where(
            mine == 0, jnp.stack([value, other], axis), jnp.stack([other, value], axis)
        )
        held.append(bit)
    return value


def scatter_bits(value, me, count, order):
    held = sorted(order, reverse=True)
    for bit in order:
        axis = held.index(bit)
        mine = (me >> bit) & 1
        send = lax.dynamic_index_in_dim(value, 1 - mine, axis, keepdims=False)
        keep = lax.dynamic_index_in_dim(value, mine, axis, keepdims=False)
        value = keep + flip(send, count, bit)
        held.remove(bit)
    return value


def bit_orders(bits):
    links = list(range(1, bits))
    head, tail = links[:-1], links[-1:]
    return [[0] + head[k:] + head[:k] + tail for k in range(3)]


def row_parts(rows):
    units = rows // 8
    cuts = [8 * (units * k // 3) for k in range(4)]
    return list(zip(cuts[:-1], cuts[1:]))


def gather_rows(block, me, count):
    bits = count.bit_length() - 1
    rows, cols = block.shape
    parts = []
    for order, (low, high) in zip(bit_orders(bits), row_parts(rows)):
        part = gather_bits(block[low:high], me, count, order[::-1])
        parts.append(part.reshape(count, high - low, cols))
    return jnp.concatenate(parts, axis=1).reshape(count * rows, cols)


def sum_rows(value, me, count):
    bits = count.bit_length() - 1
    rows, cols = value.shape[0] // count, value.shape[1]
    cube = value.reshape(count, rows, cols)
    parts = []
    for order, (low, high) in zip(bit_orders(bits), row_parts(rows)):
        part = cube[:, low:high].reshape((2,) * bits + (high - low, cols))
        part = scatter_bits(part, me, count, order)
        part = gather_bits(part, me, count, order[::-1])
        parts.append(part.reshape(count, high - low, cols))
    return jnp.concatenate(parts, axis=1).reshape(count * rows, cols)


def sum_small(value, me, count):
    bits = count.bit_length() - 1
    rows, cols = value.shape
    value = scatter_bits(value.reshape(2, rows // 2, cols), me, count, [0])
    for bit in range(1, bits):
        value = value + flip(value, count, bit)
    return gather_bits(value, me, count, [0]).reshape(rows, cols)


def on_device(weight_rows, moment_rows, grad_rows, basis, old_bounds, new_bounds):
    hosts, per_host = lax.axis_size("hst"), lax.axis_size("dev")
    count = hosts * per_host
    old_cap, cols = weight_rows.shape
    new_cap = grad_rows.shape[0]
    me = lax.axis_index("hst") * per_host + lax.axis_index("dev")

    def branch(lost, weight_rows, moment_rows, grad_rows, basis, old_bounds):
        bounds = new_ranges(lost, hosts, per_host)
        blocks = plan_blocks(bounds, old_cap, new_cap)
        first = old_bounds[me]
        owned = old_bounds[me + 1] - first
        live_count = jnp.asarray(np.diff(bounds).astype(np.int32))[me]
        live = (jnp.arange(new_cap, dtype=jnp.int32) < live_count)[:, None]

        def move(rows, scale):
            slots = jnp.arange(-BLOCK, old_cap + BLOCK, dtype=jnp.int32)[:, None]
            padded = jnp.where(
                (slots >= 0) & (slots < owned),
                jnp.pad(rows, ((BLOCK, BLOCK), (0, 0))),
                jnp.float32(0.0),
            )
            padded = lax.optimization_barrier(padded)
            out = []
            for start, rounds in blocks:
                size = min(BLOCK, -(-(new_cap - start) // 16) * 16)
                total = None
                for pairs in rounds:
                    begin = np.zeros(count, np.int32)
                    for src, dst in pairs:
                        begin[src] = bounds[dst] + start
                    offset = jnp.clip(jnp.asarray(begin)[me] - first, -BLOCK, old_cap) + BLOCK
                    send = lax.dynamic_slice_in_dim(padded, offset, size, 0)
                    send = (send * scale).astype(WIRE)
                    got = lax.ppermute(send, AXES, pairs).astype(jnp.float32)
                    total = got if total is None else total + got
                out.append(total)
            return jnp.concatenate(out, axis=0)[:new_cap] * (1.0 / scale)

        moment = move(moment_rows, MOMENT_SCALE)
        full_basis = gather_rows(basis, me, count)
        mixed = jnp.where(live, moment + grad_rows.astype(jnp.float32), jnp.float32(0.0))
        projected = jnp.dot(mixed, full_basis, precision=HIGHEST)
        gram = sum_small(jnp.dot(projected.T, projected, precision=HIGHEST), me, count)
        total = sum_rows(jnp.dot(mixed.T, projected, precision=HIGHEST), me, count)
        weight = move(weight_rows, WEIGHT_SCALE)
        factor = jnp.linalg.cholesky(gram)
        inverse = lax.linalg.triangular_solve(
            factor, jnp.eye(RANK, dtype=jnp.float32), left_side=False, lower=True, transpose_a=True
        )
        orthonormal = jnp.dot(projected, inverse, precision=HIGHEST)
        reduced = jnp.dot(total, inverse, precision=HIGHEST)
        moment_new = mixed - (1.0 - momentum_rate) * jnp.dot(
            orthonormal, reduced.T, precision=HIGHEST
        )
        column_rms = jnp.sqrt(jnp.mean(reduced * reduced, axis=0) + epsilon)
        basis_new = reduced / column_rms[None, :]
        update = jnp.dot(orthonormal, basis_new.T, precision=HIGHEST)
        weight_new = (1.0 - learn_rate * decay_rate) * weight - learn_rate * update_rms * math.sqrt(
            HIDDEN_ROWS / RANK
        ) * update
        weight_new = jnp.where(live, weight_new, jnp.float32(0.0))
        return (weight_new, moment_new, basis_new)

    edges = new_bounds[::per_host]
    lost = jnp.argmax(edges[1:] == edges[:-1]).astype(jnp.int32)
    branches = [lambda *a, l=l: branch(l, *a) for l in range(1, hosts - 1)]
    return lax.switch(
        jnp.clip(lost - 1, 0, hosts - 3),
        branches,
        weight_rows,
        moment_rows,
        grad_rows,
        basis,
        old_bounds,
    )


def solution(mesh):
    return jax.shard_map(
        on_device,
        mesh=mesh,
        in_specs=(P(AXES, None), P(AXES, None), P(AXES, None), P(AXES, None), P(), P()),
        out_specs=(P(AXES, None), P(AXES, None), P()),
        check_vma=False,
    )
```

```python
import math

import jax
import jax.numpy as jnp
import numpy as np
from jax import lax
from jax.experimental import pallas as pl
from jax.experimental.pallas import tpu as pltpu
from jax.sharding import PartitionSpec as P

HIDDEN_ROWS = 8192
RANK = 256
AXES = ("hst", "dev")
HIGHEST = lax.Precision.HIGHEST

momentum_rate = 0.6
learn_rate = 0.1
decay_rate = 0.5
update_rms = 0.2
epsilon = 1e-06

TILE = 16
CHUNK = 96
WIRE = jnp.float16
WEIGHT_SCALE = 2.0**15
MOMENT_SCALE = 2.0**13


def new_ranges(lost, hosts, per_host):
    left = (hosts - 1) * per_host
    ids = np.arange(hosts * per_host + 1)
    first = lost * per_host
    rank = np.where(ids <= first, ids, np.maximum(ids - per_host, first))
    return rank * HIDDEN_ROWS // left


def plan_rounds(bounds, old_cap):
    count = len(bounds) - 1
    even = HIDDEN_ROWS // count
    items = []
    for dst in range(count):
        for src in range(count):
            low = max(bounds[dst], src * even) - bounds[dst]
            high = min(bounds[dst + 1], src * even + old_cap, HIDDEN_ROWS) - bounds[dst]
            low = low // TILE * TILE
            while low < high:
                size = min(-(-(high - low) // TILE) * TILE, CHUNK)
                items.append((-size, src, dst, low))
                low += size
    items.sort()
    rounds = []
    for size, src, dst, slot in items:
        for held in rounds:
            if all(src != a and dst != b for _, a, b, _ in held):
                held.append((-size, src, dst, slot))
                break
        else:
            rounds.append([(-size, src, dst, slot)])
    return rounds


def pack_rows(weight_rows, moment_rows, starts, sizes):
    cap, cols = weight_rows.shape
    step = 512
    tiles = cols // step
    top = cap + CHUNK + 8

    def kernel(starts_ref, weight_ref, moment_ref, *rest):
        outs, held = rest[:-1], rest[-1]
        tile = pl.program_id(0)
        held[:CHUNK, :] = jnp.zeros((CHUNK, step), jnp.float32)
        held[CHUNK + cap :, :] = jnp.zeros((CHUNK + 8, step), jnp.float32)
        rows = lax.broadcasted_iota(jnp.int32, (cap, step), 0)
        own = rows < starts_ref[len(sizes)]

        @pl.when(tile < tiles)
        def _():
            held[CHUNK : CHUNK + cap, :] = jnp.where(own, moment_ref[...] * MOMENT_SCALE, 0.0)

        @pl.when(tile >= tiles)
        def _():
            held[CHUNK : CHUNK + cap, :] = jnp.where(own, weight_ref[...] * WEIGHT_SCALE, 0.0)

        for index, size in enumerate(sizes):
            start = starts_ref[index]
            base = pl.multiple_of(start // 8 * 8, 8)
            window = held[pl.ds(base, size + 8), :]
            shift = lax.rem(size + 8 - (start - base), size + 8)
            outs[index][...] = pltpu.roll(window, shift, 0)[:size]

    grid_spec = pltpu.PrefetchScalarGridSpec(
        num_scalar_prefetch=1,
        grid=(2 * tiles,),
        in_specs=[
            pl.BlockSpec((cap, step), lambda t, s: (0, jnp.maximum(t - tiles, 0))),
            pl.BlockSpec((cap, step), lambda t, s: (0, jnp.minimum(t, tiles - 1))),
        ],
        out_specs=[pl.BlockSpec((size, step), lambda t, s: (0, t)) for size in sizes],
        scratch_shapes=[pltpu.VMEM((top + CHUNK, step), jnp.float32)],
    )
    return pl.pallas_call(
        kernel,
        grid_spec=grid_spec,
        out_shape=[jax.ShapeDtypeStruct((size, 2 * cols), jnp.float32) for size in sizes],
        compiler_params=pltpu.CompilerParams(vmem_limit_bytes=32 * 2**20),
    )(starts, weight_rows, moment_rows)


def flip(value, count, bit):
    return lax.ppermute(value, AXES, [(i, i ^ (1 << bit)) for i in range(count)])


def gather_bits(value, me, count, order):
    held = []
    for bit in order:
        other = flip(value, count, bit)
        axis = sum(b > bit for b in held)
        mine = (me >> bit) & 1
        value = jnp.where(
            mine == 0, jnp.stack([value, other], axis), jnp.stack([other, value], axis)
        )
        held.append(bit)
    return value


def scatter_bits(value, me, count, order):
    held = sorted(order, reverse=True)
    for bit in order:
        axis = held.index(bit)
        mine = (me >> bit) & 1
        send = lax.dynamic_index_in_dim(value, 1 - mine, axis, keepdims=False)
        keep = lax.dynamic_index_in_dim(value, mine, axis, keepdims=False)
        value = keep + flip(send, count, bit)
        held.remove(bit)
    return value


def bit_orders(bits):
    links = list(range(1, bits))
    return [[0] + links, [0] + links[1::-1] + links[2:]]


def row_parts(rows):
    units = rows // 8
    cuts = [8 * (units * k // 2) for k in range(3)]
    return list(zip(cuts[:-1], cuts[1:]))


def sum_rows(value, me, count):
    bits = count.bit_length() - 1
    rows, cols = value.shape[0] // count, value.shape[1]
    cube = value.reshape(count, rows, cols)
    parts = []
    for order, (low, high) in zip(bit_orders(bits), row_parts(rows)):
        part = cube[:, low:high].reshape((2,) * bits + (high - low, cols))
        part = scatter_bits(part, me, count, order)
        part = gather_bits(part, me, count, order[::-1])
        parts.append(part.reshape(count, high - low, cols))
    return jnp.concatenate(parts, axis=1).reshape(count * rows, cols)


def on_device(weight_rows, moment_rows, grad_rows, basis, old_bounds, new_bounds):
    hosts, per_host = lax.axis_size("hst"), lax.axis_size("dev")
    count = hosts * per_host
    old_cap, cols = weight_rows.shape
    new_cap = grad_rows.shape[0]
    me = lax.axis_index("hst") * per_host + lax.axis_index("dev")

    plans = [plan_rounds(new_ranges(lost, hosts, per_host), old_cap) for lost in range(1, hosts - 1)]
    number = max(len(rounds) for rounds in plans)
    plans = [rounds + [[]] * (number - len(rounds)) for rounds in plans]
    sizes = [max(item[0] for rounds in plans for item in rounds[k]) for k in range(number)]
    table = np.zeros((hosts - 2, count, 2 * number), np.int32)
    for index, rounds in enumerate(plans):
        bounds = new_ranges(index + 1, hosts, per_host)
        for k, held in enumerate(rounds):
            for _, src, dst, slot in held:
                table[index, src, k] = bounds[dst] + slot
                table[index, dst, number + k] = slot // TILE
    edges = new_bounds[::per_host]
    lost = jnp.argmax(edges[1:] == edges[:-1]).astype(jnp.int32)
    case = jnp.clip(lost - 1, 0, hosts - 3)
    line = lax.dynamic_slice(jnp.asarray(table), (case, me, 0), (1, 1, 2 * number))[0, 0]
    old_range = lax.dynamic_slice_in_dim(old_bounds, me, 2)
    new_range = lax.dynamic_slice_in_dim(new_bounds, me, 2)
    live = (jnp.arange(new_cap, dtype=jnp.int32) < new_range[1] - new_range[0])[:, None]
    starts = jnp.clip(line[:number] - old_range[0], -CHUNK, old_cap) + CHUNK
    starts = jnp.concatenate([starts, old_range[1:] - old_range[:1]]).astype(jnp.int32)
    full_basis = lax.all_gather(basis, AXES, axis=0, tiled=True)
    packed = pack_rows(weight_rows, moment_rows, starts, sizes)
    packed = [
        value.astype(WIRE).reshape(size // TILE, TILE, 2 * cols)
        for value, size in zip(packed, sizes)
    ]

    def send(rounds):
        def branch(*values):
            return tuple(
                lax.ppermute(value, AXES, [(src, dst) for _, src, dst, _ in held])
                for value, held in zip(values, rounds)
            )

        return branch

    landed = lax.switch(case, [send(rounds) for rounds in plans], *packed)
    tiles = -(-new_cap // TILE)
    moved = jnp.zeros((tiles + CHUNK // TILE, TILE, 2 * cols), jnp.float32)
    for k, value in enumerate(landed):
        at = line[number + k]
        there = lax.dynamic_slice_in_dim(moved, at, value.shape[0], 0)
        moved = lax.dynamic_update_slice_in_dim(moved, there + value.astype(jnp.float32), at, 0)
    moved = moved.reshape(-1, 2 * cols)[:new_cap]
    moment = moved[:, :cols] * (1.0 / MOMENT_SCALE)
    weight = moved[:, cols:] * (1.0 / WEIGHT_SCALE)

    mixed = jnp.where(live, moment + grad_rows.astype(jnp.float32), jnp.float32(0.0))
    projected = jnp.dot(mixed, full_basis, precision=HIGHEST)
    total = sum_rows(jnp.dot(mixed.T, projected, precision=HIGHEST), me, count)
    gram = jnp.dot(full_basis.T, total, precision=HIGHEST)
    factor = jnp.linalg.cholesky(gram, symmetrize_input=False)
    inverse = lax.linalg.triangular_solve(
        factor, jnp.eye(RANK, dtype=jnp.float32), left_side=False, lower=True, transpose_a=True
    )
    orthonormal = jnp.dot(projected, inverse, precision=HIGHEST)
    reduced = jnp.dot(total, inverse, precision=HIGHEST)
    moment_new = mixed - (1.0 - momentum_rate) * jnp.dot(
        orthonormal, reduced.T, precision=HIGHEST
    )
    column_rms = jnp.sqrt(jnp.mean(reduced * reduced, axis=0) + epsilon)
    basis_new = reduced / column_rms[None, :]
    update = jnp.dot(orthonormal, basis_new.T, precision=HIGHEST)
    weight_new = (1.0 - learn_rate * decay_rate) * weight - learn_rate * update_rms * math.sqrt(
        HIDDEN_ROWS / RANK
    ) * update
    weight_new = jnp.where(live, weight_new, jnp.float32(0.0))
    return (weight_new, moment_new, basis_new)


def solution(mesh):
    return jax.shard_map(
        on_device,
        mesh=mesh,
        in_specs=(P(AXES, None), P(AXES, None), P(AXES, None), P(AXES, None), P(), P()),
        out_specs=(P(AXES, None), P(AXES, None), P()),
        check_vma=False,
    )
```

```python
import math

import jax
import jax.numpy as jnp
import numpy as np
from jax import lax
from jax.experimental import pallas as pl
from jax.experimental.pallas import tpu as pltpu
from jax.sharding import PartitionSpec as P

HIDDEN_ROWS = 8192
RANK = 256
AXES = ("hst", "dev")
HIGHEST = lax.Precision.HIGHEST
HIGH = lax.Precision.HIGH

momentum_rate = 0.6
learn_rate = 0.1
decay_rate = 0.5
update_rms = 0.2
epsilon = 1e-06

TILE = 8
CHUNK = 48
STEP = 512
PANEL = 64
GROUP = 16
VMEM_LIMIT = 16 * 2**20
FACTOR_LIMIT = 40 * 2**20
UPDATE_LIMIT = 60 * 2**20
WIRE = jnp.float16
WEIGHT_SCALE = 2.0**15
MOMENT_SCALE = 2.0**13


def new_ranges(lost, hosts, per_host):
    left = (hosts - 1) * per_host
    ids = np.arange(hosts * per_host + 1)
    first = lost * per_host
    rank = np.where(ids <= first, ids, np.maximum(ids - per_host, first))
    return rank * HIDDEN_ROWS // left


def plan_rounds(bounds, old_cap):
    count = len(bounds) - 1
    even = HIDDEN_ROWS // count
    items = []
    for dst in range(count):
        for src in range(count):
            low = max(bounds[dst], src * even) - bounds[dst]
            high = min(bounds[dst + 1], src * even + old_cap, HIDDEN_ROWS) - bounds[dst]
            low = low // TILE * TILE
            while low < high:
                size = min(-(-(high - low) // TILE) * TILE, CHUNK)
                items.append((-size, src, dst, low))
                low += size
    items.sort()
    rounds = []
    for size, src, dst, slot in items:
        for held in rounds:
            if all(src != a and dst != b for _, a, b, _ in held):
                held.append((-size, src, dst, slot))
                break
        else:
            rounds.append([(-size, src, dst, slot)])
    return rounds


def pack_rows(weight_rows, moment_rows, table, place, old_bounds, new_bounds, sizes, hosts):
    cap, cols = weight_rows.shape
    tiles = cols // STEP
    number = len(sizes)
    count = old_bounds.shape[0] - 1
    per_host = count // hosts

    def kernel(table_ref, place_ref, old_ref, new_ref, weight_ref, moment_ref, *rest):
        outs, (held, starts) = rest[:-2], rest[-2:]
        tile = pl.program_id(0)

        @pl.when(tile == 0)
        def _():
            me = place_ref[0]
            case = jnp.int32(0)
            for host in range(1, hosts - 1):
                empty = new_ref[host * per_host] == new_ref[(host + 1) * per_host]
                case = jnp.where(empty, host - 1, case)
            first = old_ref[me]
            starts[number] = old_ref[me + 1] - first
            for index in range(number):
                row = table_ref[(case * count + me) * number + index] - first
                starts[index] = jnp.clip(row, -CHUNK, cap) + CHUNK
            held[:CHUNK, :] = jnp.zeros((CHUNK, STEP), jnp.float32)
            held[CHUNK + cap :, :] = jnp.zeros((held.shape[0] - CHUNK - cap, STEP), jnp.float32)

        own = lax.broadcasted_iota(jnp.int32, (cap, STEP), 0) < starts[number]

        @pl.when(tile < tiles)
        def _():
            held[CHUNK : CHUNK + cap, :] = jnp.where(own, moment_ref[...] * MOMENT_SCALE, 0.0)

        @pl.when(tile >= tiles)
        def _():
            held[CHUNK : CHUNK + cap, :] = jnp.where(own, weight_ref[...] * WEIGHT_SCALE, 0.0)

        for index, size in enumerate(sizes):
            start = starts[index]
            base = pl.multiple_of(start // 8 * 8, 8)
            window = held[pl.ds(base, size + 8), :]
            shift = lax.rem(size + 8 - (start - base), size + 8)
            outs[index][...] = pltpu.roll(window, shift, 0)[:size]

    grid_spec = pltpu.PrefetchScalarGridSpec(
        num_scalar_prefetch=4,
        grid=(2 * tiles,),
        in_specs=[
            pl.BlockSpec((cap, STEP), lambda t, *_: (0, jnp.maximum(t - tiles, 0))),
            pl.BlockSpec((cap, STEP), lambda t, *_: (0, jnp.minimum(t, tiles - 1))),
        ],
        out_specs=[pl.BlockSpec((size, STEP), lambda t, *_: (0, t)) for size in sizes],
        scratch_shapes=[
            pltpu.VMEM((cap + 2 * CHUNK + 8, STEP), jnp.float32),
            pltpu.SMEM((number + 1,), jnp.int32),
        ],
    )
    return pl.pallas_call(
        kernel,
        grid_spec=grid_spec,
        out_shape=[jax.ShapeDtypeStruct((size, 2 * cols), jnp.float32) for size in sizes],
        compiler_params=pltpu.CompilerParams(vmem_limit_bytes=VMEM_LIMIT),
    )(table, place, old_bounds, new_bounds, weight_rows, moment_rows)


def split(value):
    high = value.astype(jnp.bfloat16)
    return high, (value - high.astype(jnp.float32)).astype(jnp.bfloat16)


def split_product(left, right):
    def dot(a, b):
        return jnp.dot(a, b, preferred_element_type=jnp.float32)

    return dot(left[0], right[0]) + (dot(left[0], right[1]) + dot(left[1], right[0]))


def place_rounds(total, values, slots_ref, sizes):
    for index, size in enumerate(sizes):
        at = pl.multiple_of(slots_ref[index] * TILE, TILE)
        total[pl.ds(at, size), :] += values[index][...]


def mix_and_project(landed, slots, grad_rows, basis, sizes):
    cap, cols = grad_rows.shape
    rows = -(-cap // 8) * 8
    top = -(-cap // TILE) * TILE + CHUNK

    def kernel(slots_ref, *refs):
        values, (grad_ref, basis_ref, mixed_ref, projected_ref, total) = refs[: len(sizes)], refs[len(sizes) :]
        total[...] = jnp.zeros((top, STEP), jnp.float32)
        total[:cap, :] = grad_ref[...].astype(jnp.float32) * MOMENT_SCALE
        place_rounds(total, values, slots_ref, sizes)
        live = lax.broadcasted_iota(jnp.int32, (rows, STEP), 0) < slots_ref[len(sizes)]
        mixed = jnp.where(live, total[:rows, :] * (1.0 / MOMENT_SCALE), 0.0)
        mixed_ref[...] = mixed

        @pl.when(pl.program_id(0) == 0)
        def _():
            projected_ref[...] = jnp.zeros((rows, RANK), jnp.float32)

        projected_ref[...] += split_product(split(mixed), split(basis_ref[...]))

    grid_spec = pltpu.PrefetchScalarGridSpec(
        num_scalar_prefetch=1,
        grid=(cols // STEP,),
        in_specs=[pl.BlockSpec((size, STEP), lambda t, *_: (0, t)) for size in sizes]
        + [
            pl.BlockSpec((cap, STEP), lambda t, *_: (0, t)),
            pl.BlockSpec((STEP, RANK), lambda t, *_: (t, 0)),
        ],
        out_specs=[
            pl.BlockSpec((rows, STEP), lambda t, *_: (0, t)),
            pl.BlockSpec((rows, RANK), lambda t, *_: (0, 0)),
        ],
        scratch_shapes=[pltpu.VMEM((top, STEP), jnp.float32)],
    )
    return pl.pallas_call(
        kernel,
        grid_spec=grid_spec,
        out_shape=[
            jax.ShapeDtypeStruct((rows, cols), jnp.float32),
            jax.ShapeDtypeStruct((rows, RANK), jnp.float32),
        ],
        compiler_params=pltpu.CompilerParams(vmem_limit_bytes=VMEM_LIMIT),
    )(slots, *landed, grad_rows, basis)


def update_rows(landed, slots, mixed, high, low, reduced_t, sizes, cap):
    rows, cols = mixed.shape
    top = -(-cap // TILE) * TILE + CHUNK

    def kernel(slots_ref, *refs):
        values = refs[: len(sizes)]
        mixed_ref, high_ref, low_ref, reduced_ref, weight_ref, moment_ref, total = refs[len(sizes) :]
        total[...] = jnp.zeros((top, STEP), jnp.float32)
        place_rounds(total, values, slots_ref, sizes)
        step = split_product((high_ref[...], low_ref[...]), split(reduced_ref[...]))
        live = lax.broadcasted_iota(jnp.int32, (cap, STEP), 0) < slots_ref[len(sizes)]
        kept = total[:cap, :] * ((1.0 - learn_rate * decay_rate) / WEIGHT_SCALE)
        weight_ref[...] = jnp.where(live, kept - step[rows : rows + cap], 0.0)
        moment_ref[...] = mixed_ref[:cap, :] - step[:cap]

    grid_spec = pltpu.PrefetchScalarGridSpec(
        num_scalar_prefetch=1,
        grid=(cols // STEP,),
        in_specs=[pl.BlockSpec((size, STEP), lambda t, *_: (0, t)) for size in sizes]
        + [
            pl.BlockSpec((rows, STEP), lambda t, *_: (0, t)),
            pl.BlockSpec((2 * rows, RANK), lambda t, *_: (0, 0)),
            pl.BlockSpec((2 * rows, RANK), lambda t, *_: (0, 0)),
            pl.BlockSpec((RANK, STEP), lambda t, *_: (0, t)),
        ],
        out_specs=[pl.BlockSpec((cap, STEP), lambda t, *_: (0, t))] * 2,
        scratch_shapes=[pltpu.VMEM((top, STEP), jnp.float32)],
    )
    return pl.pallas_call(
        kernel,
        grid_spec=grid_spec,
        out_shape=[jax.ShapeDtypeStruct((cap, cols), jnp.float32)] * 2,
        compiler_params=pltpu.CompilerParams(vmem_limit_bytes=UPDATE_LIMIT),
    )(slots, *landed, mixed, high, low, reduced_t)


def dot(a, b, dims):
    return lax.dot_general(a, b, dims, precision=HIGHEST, preferred_element_type=jnp.float32)


def invert_factor(left, right, out_ref):
    size = left.shape[0]
    contract = (((1,), (1,)), ((), ()))
    rows = lax.broadcasted_iota(jnp.int32, (size, size), 0)
    cols = lax.broadcasted_iota(jnp.int32, (size, size), 1)
    right[...] = jnp.where(rows == cols, 1.0, 0.0)
    row = lax.broadcasted_iota(jnp.int32, (PANEL, PANEL), 0)
    col = lax.broadcasted_iota(jnp.int32, (PANEL, PANEL), 1)
    for start in range(0, size, PANEL):
        stop = start + PANEL
        block = left[start:stop, start:stop]
        unit = jnp.where(row == col, 1.0, 0.0)
        pivots = jnp.ones((PANEL, PANEL), jnp.float32)
        for first in range(0, PANEL, GROUP):
            heads = [
                jnp.broadcast_to(block[:, k : k + 1], (PANEL, PANEL))
                for k in range(first, first + GROUP)
            ]
            for k in range(first, first + GROUP):
                head = heads[k - first]
                pivot = head[k : k + 1, :]
                ratio = jnp.where(row > k, head * (1.0 / pivot), 0.0)
                pivots = jnp.where(row == k, pivot, pivots)
                for later in range(k + 1, first + GROUP):
                    other = heads[later - first]
                    heads[later - first] = other - ratio * other[k : k + 1, :]
                if first + GROUP < PANEL:
                    block = block - ratio * block[k : k + 1, :]
                unit = unit - ratio * unit[k : k + 1, :]
        inverse = unit * lax.rsqrt(pivots)
        strip = dot(inverse, right[start:stop, :], (((1,), (0,)), ((), ())))
        out_ref[start:stop, :] = strip
        if stop < size:
            lower = dot(left[stop:, start:stop], inverse, contract)
            left[stop:, stop:] -= dot(lower, lower, contract)
            right[stop:, :] -= dot(lower, strip, (((1,), (0,)), ((), ())))


def factor_kernel(total_ref, basis_ref, projected_ref, reduced_ref, scaled_ref, high_ref, low_ref, left, right, inverse):
    rows = projected_ref.shape[0]
    plain = (((1,), (0,)), ((), ()))
    contract = (((1,), (1,)), ((), ()))
    left[...] = dot(total_ref[...], basis_ref[...], plain)
    invert_factor(left, right, inverse)
    reduced = dot(inverse[...], total_ref[...], plain)
    reduced_ref[...] = reduced
    rms = jnp.sqrt(jnp.mean(reduced * reduced, axis=1, keepdims=True) + epsilon)
    scaled_ref[...] = reduced / rms
    rate = learn_rate * update_rms * math.sqrt(HIDDEN_ROWS / RANK)
    projected = projected_ref[...]
    for_moment = dot(projected, (1.0 - momentum_rate) * inverse[...], contract)
    for_weight = dot(projected, inverse[...] * (rate / rms), contract)
    high_ref[:rows, :], low_ref[:rows, :] = split(for_moment)
    high_ref[rows:, :], low_ref[rows:, :] = split(for_weight)


def factor(total_t, basis, projected):
    rows = projected.shape[0]
    square = pltpu.VMEM((RANK, RANK), jnp.float32)
    return pl.pallas_call(
        factor_kernel,
        out_shape=[jax.ShapeDtypeStruct(total_t.shape, jnp.float32)] * 2
        + [jax.ShapeDtypeStruct((2 * rows, RANK), jnp.bfloat16)] * 2,
        scratch_shapes=[square] * 3,
        compiler_params=pltpu.CompilerParams(vmem_limit_bytes=FACTOR_LIMIT),
    )(total_t, basis, projected)


def flip(value, count, bit):
    return lax.ppermute(value, AXES, [(i, i ^ (1 << bit)) for i in range(count)])


def gather_bits(value, held, me, count, order):
    held = list(held)
    for bit in order:
        other = flip(value, count, bit)
        axis = sum(b > bit for b in held)
        mine = (me >> bit) & 1
        value = jnp.where(
            mine == 0, jnp.stack([value, other], axis), jnp.stack([other, value], axis)
        )
        held.append(bit)
    return value


def scatter_bits(value, held, me, count, order):
    held = sorted(held, reverse=True)
    for bit in order:
        axis = held.index(bit)
        mine = (me >> bit) & 1
        send = lax.dynamic_index_in_dim(value, 1 - mine, axis, keepdims=False)
        keep = lax.dynamic_index_in_dim(value, mine, axis, keepdims=False)
        value = keep + flip(send, count, bit)
        held.remove(bit)
    return value


def scatter_all(value, me, count):
    bits = count.bit_length() - 1
    rows, cols = value.shape
    half = cols // 2
    links, rest = list(range(1, bits)), list(range(3, bits))
    cube = value.reshape((2,) * bits + (rows // count, cols))
    cube = scatter_bits(cube, range(bits), me, count, [0])
    near = scatter_bits(cube[..., :half], links, me, count, [1, 2])
    far = scatter_bits(cube[..., half:], links, me, count, [2, 1])
    cube = jnp.concatenate([near, far], axis=-1)
    cube = scatter_bits(cube, rest, me, count, rest[:-1])
    return cube + flip(cube, count, rest[-1])


def gather_all(block, held, me, count):
    bits = count.bit_length() - 1
    half = block.shape[-1] // 2
    links, rest = list(range(1, bits)), list(range(3, bits))
    cube = gather_bits(block, held, me, count, [bit for bit in rest[::-1] if bit not in held])
    near = gather_bits(cube[..., :half], rest, me, count, [2, 1])
    far = gather_bits(cube[..., half:], rest, me, count, [1, 2])
    cube = jnp.concatenate([near, far], axis=-1)
    return gather_bits(cube, links, me, count, [0]).reshape(-1, block.shape[-1])


def on_device(weight_rows, moment_rows, grad_rows, basis, old_bounds, new_bounds):
    hosts, per_host = lax.axis_size("hst"), lax.axis_size("dev")
    count = hosts * per_host
    old_cap, cols = weight_rows.shape
    new_cap = grad_rows.shape[0]
    me = lax.axis_index("hst") * per_host + lax.axis_index("dev")

    plans = [plan_rounds(new_ranges(lost, hosts, per_host), old_cap) for lost in range(1, hosts - 1)]
    number = max(len(rounds) for rounds in plans)
    plans = [rounds + [[]] * (number - len(rounds)) for rounds in plans]
    sizes = [max(item[0] for rounds in plans for item in rounds[k]) for k in range(number)]
    sizes = [-(-size // 16) * 16 for size in sizes]
    first_rows = np.zeros((hosts - 2, count, number), np.int32)
    slot_tiles = np.zeros((hosts - 2, count, number), np.int32)
    for index, rounds in enumerate(plans):
        bounds = new_ranges(index + 1, hosts, per_host)
        for k, held in enumerate(rounds):
            for _, src, dst, slot in held:
                first_rows[index, src, k] = bounds[dst] + slot
                slot_tiles[index, dst, k] = slot // TILE

    place = jnp.full((1,), me, jnp.int32)
    packed = pack_rows(
        weight_rows,
        moment_rows,
        jnp.asarray(first_rows.reshape(-1)),
        place,
        old_bounds,
        new_bounds,
        sizes,
        hosts,
    )
    packed = [value.astype(WIRE) for value in packed]

    edges = new_bounds[::per_host]
    lost = jnp.argmax(edges[1:] == edges[:-1]).astype(jnp.int32)
    case = jnp.clip(lost - 1, 0, hosts - 3)

    def send(rounds):
        def branch(basis, *values):
            landed = [
                lax.ppermute(value, AXES, [(src, dst) for _, src, dst, _ in held])
                for value, held in zip(values, rounds)
            ]
            return (gather_all(basis, [], me, count), *landed)

        return branch

    full_basis, *landed = lax.switch(case, [send(rounds) for rounds in plans], basis, *packed)
    line = lax.dynamic_slice(jnp.asarray(slot_tiles), (case, me, 0), (1, 1, number))[0, 0]
    new_range = lax.dynamic_slice_in_dim(new_bounds, me, 2)
    slots = jnp.concatenate([line, new_range[1:] - new_range[:1]])

    moments = [value[:, :cols].astype(jnp.float32) for value in landed]
    mixed, projected = mix_and_project(moments, slots, grad_rows, full_basis, sizes)
    local = jnp.dot(projected.T, mixed, precision=HIGH)
    last = count.bit_length() - 2
    total_t = gather_all(scatter_all(local, me, count), [last], me, count)
    reduced_t, scaled_t, high, low = factor(total_t, full_basis, projected)
    weights = [value[:, cols:].astype(jnp.float32) for value in landed]
    weight_new, moment_new = update_rows(
        weights, slots, mixed, high, low, reduced_t, sizes, new_cap
    )
    return (weight_new, moment_new, scaled_t.T)


def solution(mesh):
    return jax.shard_map(
        on_device,
        mesh=mesh,
        in_specs=(P(AXES, None), P(AXES, None), P(AXES, None), P(AXES, None), P(), P()),
        out_specs=(P(AXES, None), P(AXES, None), P()),
        check_vma=False,
    )
```

```python
import math

import jax
import jax.numpy as jnp
import numpy as np
from jax import lax
from jax.experimental import pallas as pl
from jax.experimental.pallas import tpu as pltpu
from jax.sharding import PartitionSpec as P

HIDDEN_ROWS = 8192
RANK = 256
AXES = ("hst", "dev")
HIGHEST = lax.Precision.HIGHEST
HIGH = lax.Precision.HIGH

momentum_rate = 0.6
learn_rate = 0.1
decay_rate = 0.5
update_rms = 0.2
epsilon = 1e-06

TILE = 8
SIZES = (144, 96, 80, 64, 48)
STEP = 512
PANEL = 64
GROUP = 16
VMEM_LIMIT = 16 * 2**20
FACTOR_LIMIT = 60 * 2**20
UPDATE_LIMIT = 60 * 2**20
WIRE = jnp.float16
WEIGHT_SCALE = 2.0**15
MOMENT_SCALE = 2.0**13


def new_ranges(lost, hosts, per_host):
    left = (hosts - 1) * per_host
    ids = np.arange(hosts * per_host + 1)
    first = lost * per_host
    rank = np.where(ids <= first, ids, np.maximum(ids - per_host, first))
    return rank * HIDDEN_ROWS // left


def row_windows(bounds, old_cap):
    count = len(bounds) - 1
    even = HIDDEN_ROWS // count
    windows = []
    for dst in range(count):
        for src in range(count):
            low = max(bounds[dst], src * even) - bounds[dst]
            high = min(bounds[dst + 1], src * even + old_cap, HIDDEN_ROWS) - bounds[dst]
            if low < high:
                windows.append((dst, src, int(low) // TILE * TILE, int(high)))
    return windows


def plan_greedy(bounds, old_cap, sizes):
    rounds = []
    for dst, src, low, high in row_windows(bounds, old_cap):
        while low < high:
            for held in rounds:
                if all(src != a and dst != b for a, b, _ in held):
                    break
            else:
                held = []
                rounds.append(held)
            held.append((src, dst, low))
            low += sizes[0]
    return rounds


def plan_chain(bounds, old_cap, sizes, per_host):
    windows = row_windows(bounds, old_cap)
    number = len(sizes)
    totals = [sum(sizes[k] for k in range(number) if m >> k & 1) for m in range(1 << number)]
    states, trail = {(0, 0): (0.0, None, 0)}, []
    last_dst = last_src = None
    for dst, src, low, high in windows:
        need = high - low
        sets = [
            m
            for m in range(1, 1 << number)
            if totals[m] >= need
            and all(totals[m] - sizes[k] < need for k in range(number) if m >> k & 1)
        ]
        weight = 0.01 + (src // per_host != dst // per_host)
        following = {}
        for state, (cost, _, _) in states.items():
            at_dst = state[0] if dst == last_dst else 0
            at_src = state[1] if src == last_src else 0
            for m in sets:
                if m & (at_dst | at_src):
                    continue
                key, price = (at_dst | m, at_src | m), cost + weight * totals[m]
                if key not in following or price < following[key][0]:
                    following[key] = (price, state, m)
        if not following:
            return None
        trail.append(following)
        states, last_dst, last_src = following, dst, src
    state = min(states, key=lambda key: (states[key][0], key))
    rounds = [[] for _ in sizes]
    for (dst, src, low, _), following in zip(windows[::-1], trail[::-1]):
        _, previous, m = following[state]
        for k in range(number):
            if m >> k & 1:
                rounds[k].append((src, dst, low))
                low += sizes[k]
        state = previous
    for held in rounds:
        if len({a for a, _, _ in held}) < len(held) or len({b for _, b, _ in held}) < len(held):
            return None
    return rounds


def pack_rows(weight_rows, moment_rows, table, place, old_bounds, new_bounds, sizes, hosts):
    cap, cols = weight_rows.shape
    tiles = cols // STEP
    number = len(sizes)
    widest = max(sizes)
    count = old_bounds.shape[0] - 1
    per_host = count // hosts

    def kernel(table_ref, place_ref, old_ref, new_ref, weight_ref, moment_ref, *rest):
        outs, (held, starts) = rest[:-2], rest[-2:]
        tile = pl.program_id(0)

        @pl.when(tile == 0)
        def _():
            me = place_ref[0]
            case = jnp.int32(0)
            for host in range(1, hosts - 1):
                empty = new_ref[host * per_host] == new_ref[(host + 1) * per_host]
                case = jnp.where(empty, host - 1, case)
            first = old_ref[me]
            starts[number] = old_ref[me + 1] - first
            for index in range(number):
                row = table_ref[(case * count + me) * number + index] - first
                starts[index] = jnp.clip(row, -widest, cap) + widest
            held[:widest, :] = jnp.zeros((widest, STEP), jnp.float32)
            held[widest + cap :, :] = jnp.zeros((held.shape[0] - widest - cap, STEP), jnp.float32)

        own = lax.broadcasted_iota(jnp.int32, (cap, STEP), 0) < starts[number]

        @pl.when(tile < tiles)
        def _():
            held[widest : widest + cap, :] = jnp.where(own, moment_ref[...] * MOMENT_SCALE, 0.0)

        @pl.when(tile >= tiles)
        def _():
            held[widest : widest + cap, :] = jnp.where(own, weight_ref[...] * WEIGHT_SCALE, 0.0)

        for index, size in enumerate(sizes):
            start = starts[index]
            base = pl.multiple_of(start // 8 * 8, 8)
            window = held[pl.ds(base, size + 8), :]
            shift = lax.rem(size + 8 - (start - base), size + 8)
            outs[index][...] = pltpu.roll(window, shift, 0)[:size]

    grid_spec = pltpu.PrefetchScalarGridSpec(
        num_scalar_prefetch=4,
        grid=(2 * tiles,),
        in_specs=[
            pl.BlockSpec((cap, STEP), lambda t, *_: (0, jnp.maximum(t - tiles, 0))),
            pl.BlockSpec((cap, STEP), lambda t, *_: (0, jnp.minimum(t, tiles - 1))),
        ],
        out_specs=[pl.BlockSpec((size, STEP), lambda t, *_: (0, t)) for size in sizes],
        scratch_shapes=[
            pltpu.VMEM((cap + 2 * widest + 8, STEP), jnp.float32),
            pltpu.SMEM((number + 1,), jnp.int32),
        ],
    )
    return pl.pallas_call(
        kernel,
        grid_spec=grid_spec,
        out_shape=[jax.ShapeDtypeStruct((size, 2 * cols), jnp.float32) for size in sizes],
        cost_estimate=pl.CostEstimate(
            flops=0, bytes_accessed=int(8 * (cap + sum(sizes)) * cols), transcendentals=0
        ),
        compiler_params=pltpu.CompilerParams(vmem_limit_bytes=VMEM_LIMIT),
    )(table, place, old_bounds, new_bounds, weight_rows, moment_rows)


def split(value):
    high = value.astype(jnp.bfloat16)
    return high, (value - high.astype(jnp.float32)).astype(jnp.bfloat16)


def split_product(left, right):
    def dot(a, b):
        return jnp.dot(a, b, preferred_element_type=jnp.float32)

    return dot(left[0], right[0]) + (dot(left[0], right[1]) + dot(left[1], right[0]))


def place_rounds(total, values, slots_ref, sizes):
    for index, size in enumerate(sizes):
        at = pl.multiple_of(slots_ref[index] * TILE, TILE)
        total[pl.ds(at, size), :] += values[index][...]


def mix_and_project(landed, slots, grad_rows, basis, sizes):
    cap, cols = grad_rows.shape
    rows = -(-cap // 8) * 8
    top = -(-cap // TILE) * TILE + max(sizes)

    def kernel(slots_ref, *refs):
        values, (grad_ref, basis_ref, mixed_ref, projected_ref, total) = refs[: len(sizes)], refs[len(sizes) :]
        total[...] = jnp.zeros((top, STEP), jnp.float32)
        total[:cap, :] = grad_ref[...].astype(jnp.float32) * MOMENT_SCALE
        place_rounds(total, values, slots_ref, sizes)
        live = lax.broadcasted_iota(jnp.int32, (rows, STEP), 0) < slots_ref[len(sizes)]
        mixed = jnp.where(live, total[:rows, :] * (1.0 / MOMENT_SCALE), 0.0)
        mixed_ref[...] = mixed

        @pl.when(pl.program_id(0) == 0)
        def _():
            projected_ref[...] = jnp.zeros((rows, RANK), jnp.float32)

        projected_ref[...] += split_product(split(mixed), split(basis_ref[...]))

    grid_spec = pltpu.PrefetchScalarGridSpec(
        num_scalar_prefetch=1,
        grid=(cols // STEP,),
        in_specs=[pl.BlockSpec((size, STEP), lambda t, *_: (0, t)) for size in sizes]
        + [
            pl.BlockSpec((cap, STEP), lambda t, *_: (0, t)),
            pl.BlockSpec((STEP, RANK), lambda t, *_: (t, 0)),
        ],
        out_specs=[
            pl.BlockSpec((rows, STEP), lambda t, *_: (0, t)),
            pl.BlockSpec((rows, RANK), lambda t, *_: (0, 0)),
        ],
        scratch_shapes=[pltpu.VMEM((top, STEP), jnp.float32)],
    )
    return pl.pallas_call(
        kernel,
        grid_spec=grid_spec,
        out_shape=[
            jax.ShapeDtypeStruct((rows, cols), jnp.float32),
            jax.ShapeDtypeStruct((rows, RANK), jnp.float32),
        ],
        compiler_params=pltpu.CompilerParams(vmem_limit_bytes=VMEM_LIMIT),
    )(slots, *landed, grad_rows, basis)


def update_rows(landed, slots, mixed, high, low, reduced_t, rms, sizes, cap):
    rows, cols = mixed.shape
    top = -(-cap // TILE) * TILE + max(sizes)

    def kernel(slots_ref, *refs):
        values = refs[: len(sizes)]
        mixed_ref, high_ref, low_ref, reduced_ref, rms_ref = refs[len(sizes) : len(sizes) + 5]
        weight_ref, moment_ref, scaled_ref, total = refs[len(sizes) + 5 :]
        total[...] = jnp.zeros((top, STEP), jnp.float32)
        place_rounds(total, values, slots_ref, sizes)
        reduced = reduced_ref[...]
        scaled_ref[...] = (reduced / rms_ref[:, :1]).T
        step = split_product((high_ref[...], low_ref[...]), split(reduced))
        live = lax.broadcasted_iota(jnp.int32, (cap, STEP), 0) < slots_ref[len(sizes)]
        kept = total[:cap, :] * ((1.0 - learn_rate * decay_rate) / WEIGHT_SCALE)
        weight_ref[...] = jnp.where(live, kept - step[rows : rows + cap], 0.0)
        moment_ref[...] = mixed_ref[:cap, :] - step[:cap]

    grid_spec = pltpu.PrefetchScalarGridSpec(
        num_scalar_prefetch=1,
        grid=(cols // STEP,),
        in_specs=[pl.BlockSpec((size, STEP), lambda t, *_: (0, t)) for size in sizes]
        + [
            pl.BlockSpec((rows, STEP), lambda t, *_: (0, t)),
            pl.BlockSpec((2 * rows, RANK), lambda t, *_: (0, 0)),
            pl.BlockSpec((2 * rows, RANK), lambda t, *_: (0, 0)),
            pl.BlockSpec((RANK, STEP), lambda t, *_: (0, t)),
            pl.BlockSpec((RANK, 128), lambda t, *_: (0, 0)),
        ],
        out_specs=[pl.BlockSpec((cap, STEP), lambda t, *_: (0, t))] * 2
        + [pl.BlockSpec((STEP, RANK), lambda t, *_: (t, 0))],
        scratch_shapes=[pltpu.VMEM((top, STEP), jnp.float32)],
    )
    return pl.pallas_call(
        kernel,
        grid_spec=grid_spec,
        out_shape=[jax.ShapeDtypeStruct((cap, cols), jnp.float32)] * 2
        + [jax.ShapeDtypeStruct((cols, RANK), jnp.float32)],
        compiler_params=pltpu.CompilerParams(vmem_limit_bytes=UPDATE_LIMIT),
    )(slots, *landed, mixed, high, low, reduced_t, rms)


def dot(a, b, dims):
    return lax.dot_general(a, b, dims, precision=HIGHEST, preferred_element_type=jnp.float32)


def invert_factor(left, right, out_ref):
    size = left.shape[0]
    contract = (((1,), (1,)), ((), ()))
    rows = lax.broadcasted_iota(jnp.int32, (size, size), 0)
    cols = lax.broadcasted_iota(jnp.int32, (size, size), 1)
    right[...] = jnp.where(rows == cols, 1.0, 0.0)
    row = lax.broadcasted_iota(jnp.int32, (PANEL, PANEL), 0)
    col = lax.broadcasted_iota(jnp.int32, (PANEL, PANEL), 1)
    for start in range(0, size, PANEL):
        stop = start + PANEL
        block = left[start:stop, start:stop]
        unit = jnp.where(row == col, 1.0, 0.0)
        pivots = jnp.ones((PANEL, PANEL), jnp.float32)
        for first in range(0, PANEL, GROUP):
            heads = [
                jnp.broadcast_to(block[:, k : k + 1], (PANEL, PANEL))
                for k in range(first, first + GROUP)
            ]
            for k in range(first, first + GROUP):
                head = heads[k - first]
                pivot = head[k : k + 1, :]
                ratio = jnp.where(row > k, head * (1.0 / pivot), 0.0)
                pivots = jnp.where(row == k, pivot, pivots)
                for later in range(k + 1, first + GROUP):
                    other = heads[later - first]
                    heads[later - first] = other - ratio * other[k : k + 1, :]
                if first + GROUP < PANEL:
                    block = block - ratio * block[k : k + 1, :]
                unit = unit - ratio * unit[k : k + 1, :]
        inverse = unit * lax.rsqrt(pivots)
        strip = dot(inverse, right[start:stop, :], (((1,), (0,)), ((), ())))
        out_ref[start:stop, :] = strip
        if stop < size:
            lower = dot(left[stop:, start:stop], inverse, contract)
            left[stop:, stop:] -= dot(lower, lower, contract)
            right[stop:, :] -= dot(lower, strip, (((1,), (0,)), ((), ())))


def factor_kernel(core_ref, mine_ref, other_ref, basis_ref, projected_ref, *refs):
    reduced_ref, rms_ref, high_ref, low_ref, left, right, inverse, total_ref = refs
    rows = projected_ref.shape[0]
    half = mine_ref.shape[0]
    mine_at = pl.multiple_of(core_ref[0] * half, half)
    other_at = pl.multiple_of((1 - core_ref[0]) * half, half)
    total_ref[pl.ds(mine_at, half), :] = mine_ref[...]
    total_ref[pl.ds(other_at, half), :] = other_ref[...]
    plain = (((1,), (0,)), ((), ()))
    contract = (((1,), (1,)), ((), ()))
    left[...] = dot(total_ref[...], basis_ref[...], plain)
    invert_factor(left, right, inverse)
    reduced = split_product(split(inverse[...]), split(total_ref[...]))
    reduced_ref[...] = reduced
    rms = jnp.sqrt(jnp.mean(reduced * reduced, axis=1, keepdims=True) + epsilon)
    rms_ref[...] = jnp.broadcast_to(rms, rms_ref.shape)
    rate = learn_rate * update_rms * math.sqrt(HIDDEN_ROWS / RANK)
    projected = projected_ref[...]
    for_moment = dot(projected, (1.0 - momentum_rate) * inverse[...], contract)
    for_weight = dot(projected, inverse[...] * (rate / rms), contract)
    high_ref[:rows, :], low_ref[:rows, :] = split(for_moment)
    high_ref[rows:, :], low_ref[rows:, :] = split(for_weight)


def factor(core, mine, other, basis, projected):
    rows = projected.shape[0]
    cols = mine.shape[1]
    square = pltpu.VMEM((RANK, RANK), jnp.float32)
    return pl.pallas_call(
        factor_kernel,
        in_specs=[pl.BlockSpec(memory_space=pltpu.SMEM)]
        + [pl.BlockSpec(memory_space=pltpu.VMEM)] * 4,
        out_shape=[
            jax.ShapeDtypeStruct((RANK, cols), jnp.float32),
            jax.ShapeDtypeStruct((RANK, 128), jnp.float32),
        ]
        + [jax.ShapeDtypeStruct((2 * rows, RANK), jnp.bfloat16)] * 2,
        scratch_shapes=[square] * 3 + [pltpu.VMEM((RANK, cols), jnp.float32)],
        compiler_params=pltpu.CompilerParams(vmem_limit_bytes=FACTOR_LIMIT),
    )(core, mine, other, basis, projected)


def flip(value, count, bit):
    return lax.ppermute(value, AXES, [(i, i ^ (1 << bit)) for i in range(count)])


def after(value, stage):
    if stage is None:
        return value
    first = stage.reshape(-1)[0].astype(jnp.float32)
    return value + jnp.minimum(jnp.abs(first), 0.0)


def gather_bits(value, held, me, count, order):
    held = list(held)
    for bit in order:
        other = flip(value, count, bit)
        axis = sum(b > bit for b in held)
        mine = (me >> bit) & 1
        value = jnp.where(
            mine == 0, jnp.stack([value, other], axis), jnp.stack([other, value], axis)
        )
        held.append(bit)
    return value


def scatter_bits(value, held, me, count, order):
    held = sorted(held, reverse=True)
    for bit in order:
        axis = held.index(bit)
        mine = (me >> bit) & 1
        send = lax.dynamic_index_in_dim(value, 1 - mine, axis, keepdims=False)
        keep = lax.dynamic_index_in_dim(value, mine, axis, keepdims=False)
        value = keep + flip(send, count, bit)
        held.remove(bit)
    return value


def sum_chips(value, me, count):
    bits = count.bit_length() - 1
    rows, cols = value.shape
    half = cols // 2
    links, rest = list(range(1, bits)), list(range(3, bits))
    cube = value.reshape((2,) * (bits - 1) + (2 * rows // count, cols))
    near = scatter_bits(cube[..., :half], links, me, count, [1, 2])
    far = scatter_bits(cube[..., half:], links, me, count, [2, 1])
    cube = jnp.concatenate([near, far], axis=-1)
    cube = scatter_bits(cube, rest, me, count, rest[:-1])
    cube = cube + flip(cube, count, rest[-1])
    return gather_chips(cube, rest[-1:], me, count).reshape(rows, cols)


def gather_chips(block, held, me, count, stage=None):
    bits = count.bit_length() - 1
    half = block.shape[-1] // 2
    rest = list(range(3, bits))
    cube = gather_bits(block, held, me, count, [bit for bit in rest[::-1] if bit not in held])
    near = gather_bits(cube[..., :half], rest, me, count, [2])
    far = gather_bits(cube[..., half:], rest, me, count, [1])
    near = gather_bits(after(near, stage), rest + [2], me, count, [1])
    far = gather_bits(after(far, stage), rest + [1], me, count, [2])
    return jnp.concatenate([near, far], axis=-1)


def on_device(weight_rows, moment_rows, grad_rows, basis, old_bounds, new_bounds):
    hosts, per_host = lax.axis_size("hst"), lax.axis_size("dev")
    count = hosts * per_host
    old_cap, cols = weight_rows.shape
    new_cap = grad_rows.shape[0]
    me = lax.axis_index("hst") * per_host + lax.axis_index("dev")

    ranges = [new_ranges(lost, hosts, per_host) for lost in range(1, hosts - 1)]
    sizes = SIZES
    plans = [plan_chain(bounds, old_cap, sizes, per_host) for bounds in ranges]
    if any(rounds is None for rounds in plans):
        sizes = (-(-old_cap // 16) * 16,)
        plans = [plan_greedy(bounds, old_cap, sizes) for bounds in ranges]
        sizes = sizes * max(len(rounds) for rounds in plans)
    number = len(sizes)
    plans = [rounds + [[]] * (number - len(rounds)) for rounds in plans]
    first_rows = np.zeros((hosts - 2, count, number), np.int32)
    slot_tiles = np.zeros((hosts - 2, count, number), np.int32)
    for index, rounds in enumerate(plans):
        bounds = new_ranges(index + 1, hosts, per_host)
        for k, held in enumerate(rounds):
            for src, dst, slot in held:
                first_rows[index, src, k] = bounds[dst] + slot
                slot_tiles[index, dst, k] = slot // TILE

    bits = count.bit_length() - 1
    place = jnp.full((1,), me, jnp.int32)
    packed = pack_rows(
        weight_rows,
        moment_rows,
        jnp.asarray(first_rows.reshape(-1)),
        place,
        old_bounds,
        new_bounds,
        sizes,
        hosts,
    )
    full_basis = gather_chips(basis, [], me, count, packed[0])
    full_basis = gather_bits(full_basis, range(1, bits), me, count, [0]).reshape(cols, RANK)

    edges = new_bounds[::per_host]
    lost = jnp.argmax(edges[1:] == edges[:-1]).astype(jnp.int32)
    case = jnp.clip(lost - 1, 0, hosts - 3)

    def send(rounds):
        def branch(*values):
            landed = [
                lax.ppermute(value.astype(WIRE), AXES, [(src, dst) for src, dst, _ in held])
                for value, held in zip(values, rounds)
            ]
            moments = [value[:, :cols].astype(jnp.float32) for value in landed]
            weights = [value[:, cols:].astype(jnp.float32) for value in landed]
            return (*moments, *weights)

        return branch

    case = case + after(jnp.zeros((), jnp.float32), full_basis).astype(jnp.int32)
    landed = lax.switch(case, [send(rounds) for rounds in plans], *packed)
    moments, weights = landed[:number], landed[number:]
    line = lax.dynamic_slice(jnp.asarray(slot_tiles), (case, me, 0), (1, 1, number))[0, 0]
    new_range = lax.dynamic_slice_in_dim(new_bounds, me, 2)
    slots = jnp.concatenate([line, new_range[1:] - new_range[:1]])

    mixed, projected = mix_and_project(moments, slots, grad_rows, full_basis, sizes)

    def part(number):
        factor_part = lax.dynamic_slice_in_dim(projected, number * (RANK // 2), RANK // 2, 1)
        return jnp.dot(factor_part.T, mixed, precision=HIGH)

    away = flip(part(1 - (me & 1)), count, 0)
    kept = lax.optimization_barrier(part(me & 1))
    mine = sum_chips(kept + away, me, count)
    other = flip(mine, count, 0)
    core = jnp.full((1,), me & 1, jnp.int32)
    reduced_t, rms, high, low = factor(core, mine, other, full_basis, projected)
    return tuple(update_rows(weights, slots, mixed, high, low, reduced_t, rms, sizes, new_cap))


def solution(mesh):
    return jax.shard_map(
        on_device,
        mesh=mesh,
        in_specs=(P(AXES, None), P(AXES, None), P(AXES, None), P(AXES, None), P(), P()),
        out_specs=(P(AXES, None), P(AXES, None), P()),
        check_vma=False,
    )
```

```python
import math

import jax
import jax.numpy as jnp
import numpy as np
from jax import lax
from jax.experimental import pallas as pl
from jax.experimental.pallas import tpu as pltpu
from jax.sharding import PartitionSpec as P

HIDDEN_ROWS = 8192
RANK = 256
AXES = ("hst", "dev")
HIGHEST = lax.Precision.HIGHEST
HIGH = lax.Precision.HIGH

momentum_rate = 0.6
learn_rate = 0.1
decay_rate = 0.5
update_rms = 0.2
epsilon = 1e-06

TILE = 8
SIZES = (144, 96, 80, 64, 48)
STEP = 512
PANEL = 64
GROUP = 16
VMEM_LIMIT = 16 * 2**20
FINISH_LIMIT = 60 * 2**20
WIRE = jnp.float16
WEIGHT_SCALE = 2.0**15
MOMENT_SCALE = 2.0**13


def new_ranges(lost, hosts, per_host):
    left = (hosts - 1) * per_host
    ids = np.arange(hosts * per_host + 1)
    first = lost * per_host
    rank = np.where(ids <= first, ids, np.maximum(ids - per_host, first))
    return rank * HIDDEN_ROWS // left


def row_windows(bounds, old_cap):
    count = len(bounds) - 1
    even = HIDDEN_ROWS // count
    windows = []
    for dst in range(count):
        for src in range(count):
            low = max(bounds[dst], src * even) - bounds[dst]
            high = min(bounds[dst + 1], src * even + old_cap, HIDDEN_ROWS) - bounds[dst]
            if low < high:
                windows.append((dst, src, int(low) // TILE * TILE, int(high)))
    return windows


def plan_greedy(bounds, old_cap, sizes):
    rounds = []
    for dst, src, low, high in row_windows(bounds, old_cap):
        while low < high:
            for held in rounds:
                if all(src != a and dst != b for a, b, _ in held):
                    break
            else:
                held = []
                rounds.append(held)
            held.append((src, dst, low))
            low += sizes[0]
    return rounds


def plan_chain(bounds, old_cap, sizes, per_host):
    windows = row_windows(bounds, old_cap)
    number = len(sizes)
    totals = [sum(sizes[k] for k in range(number) if m >> k & 1) for m in range(1 << number)]
    states, trail = {(0, 0): (0.0, None, 0)}, []
    last_dst = last_src = None
    for dst, src, low, high in windows:
        need = high - low
        sets = [
            m
            for m in range(1, 1 << number)
            if totals[m] >= need
            and all(totals[m] - sizes[k] < need for k in range(number) if m >> k & 1)
        ]
        weight = 0.01 + (src // per_host != dst // per_host)
        following = {}
        for state, (cost, _, _) in states.items():
            at_dst = state[0] if dst == last_dst else 0
            at_src = state[1] if src == last_src else 0
            for m in sets:
                if m & (at_dst | at_src):
                    continue
                key, price = (at_dst | m, at_src | m), cost + weight * totals[m]
                if key not in following or price < following[key][0]:
                    following[key] = (price, state, m)
        if not following:
            return None
        trail.append(following)
        states, last_dst, last_src = following, dst, src
    state = min(states, key=lambda key: (states[key][0], key))
    rounds = [[] for _ in sizes]
    for (dst, src, low, _), following in zip(windows[::-1], trail[::-1]):
        _, previous, m = following[state]
        for k in range(number):
            if m >> k & 1:
                rounds[k].append((src, dst, low))
                low += sizes[k]
        state = previous
    for held in rounds:
        if len({a for a, _, _ in held}) < len(held) or len({b for _, b, _ in held}) < len(held):
            return None
    return rounds


def pack_rows(weight_rows, moment_rows, table, place, old_bounds, new_bounds, sizes, hosts):
    cap, cols = weight_rows.shape
    tiles = cols // STEP
    number = len(sizes)
    widest = max(sizes)
    count = old_bounds.shape[0] - 1
    per_host = count // hosts

    def kernel(table_ref, place_ref, old_ref, new_ref, weight_ref, moment_ref, *rest):
        outs, (held, starts) = rest[:-2], rest[-2:]
        tile = pl.program_id(0)

        @pl.when(tile == 0)
        def _():
            me = place_ref[0]
            case = jnp.int32(0)
            for host in range(1, hosts - 1):
                empty = new_ref[host * per_host] == new_ref[(host + 1) * per_host]
                case = jnp.where(empty, host - 1, case)
            first = old_ref[me]
            starts[number] = old_ref[me + 1] - first
            for index in range(number):
                row = table_ref[(case * count + me) * number + index] - first
                starts[index] = jnp.clip(row, -widest, cap) + widest
            held[:widest, :] = jnp.zeros((widest, STEP), jnp.float32)
            held[widest + cap :, :] = jnp.zeros((held.shape[0] - widest - cap, STEP), jnp.float32)

        own = lax.broadcasted_iota(jnp.int32, (cap, STEP), 0) < starts[number]

        @pl.when(tile < tiles)
        def _():
            held[widest : widest + cap, :] = jnp.where(own, moment_ref[...] * MOMENT_SCALE, 0.0)

        @pl.when(tile >= tiles)
        def _():
            held[widest : widest + cap, :] = jnp.where(own, weight_ref[...] * WEIGHT_SCALE, 0.0)

        for index, size in enumerate(sizes):
            start = starts[index]
            base = pl.multiple_of(start // 8 * 8, 8)
            window = held[pl.ds(base, size + 8), :]
            shift = lax.rem(size + 8 - (start - base), size + 8)
            outs[index][...] = pltpu.roll(window, shift, 0)[:size]

    grid_spec = pltpu.PrefetchScalarGridSpec(
        num_scalar_prefetch=4,
        grid=(2 * tiles,),
        in_specs=[
            pl.BlockSpec((cap, STEP), lambda t, *_: (0, jnp.maximum(t - tiles, 0))),
            pl.BlockSpec((cap, STEP), lambda t, *_: (0, jnp.minimum(t, tiles - 1))),
        ],
        out_specs=[pl.BlockSpec((size, STEP), lambda t, *_: (0, t)) for size in sizes],
        scratch_shapes=[
            pltpu.VMEM((cap + 2 * widest + 8, STEP), jnp.float32),
            pltpu.SMEM((number + 1,), jnp.int32),
        ],
    )
    return pl.pallas_call(
        kernel,
        grid_spec=grid_spec,
        out_shape=[jax.ShapeDtypeStruct((size, 2 * cols), jnp.float32) for size in sizes],
        cost_estimate=pl.CostEstimate(
            flops=0, bytes_accessed=int(8 * (cap + sum(sizes)) * cols), transcendentals=0
        ),
        compiler_params=pltpu.CompilerParams(vmem_limit_bytes=VMEM_LIMIT),
    )(table, place, old_bounds, new_bounds, weight_rows, moment_rows)


def split(value):
    high = value.astype(jnp.bfloat16)
    return high, (value - high.astype(jnp.float32)).astype(jnp.bfloat16)


def split_product(left, right):
    def dot(a, b):
        return jnp.dot(a, b, preferred_element_type=jnp.float32)

    return dot(left[0], right[0]) + (dot(left[0], right[1]) + dot(left[1], right[0]))


def place_rounds(total, values, slots_ref, sizes):
    for index, size in enumerate(sizes):
        at = pl.multiple_of(slots_ref[index] * TILE, TILE)
        total[pl.ds(at, size), :] += values[index][...]


def mix_and_project(landed, slots, grad_rows, basis, sizes):
    cap, cols = grad_rows.shape
    rows = -(-cap // 8) * 8
    top = -(-cap // TILE) * TILE + max(sizes)

    def kernel(slots_ref, *refs):
        values, (grad_ref, basis_ref, mixed_ref, projected_ref, total) = refs[: len(sizes)], refs[len(sizes) :]
        total[...] = jnp.zeros((top, STEP), jnp.float32)
        total[:cap, :] = grad_ref[...].astype(jnp.float32) * MOMENT_SCALE
        place_rounds(total, values, slots_ref, sizes)
        live = lax.broadcasted_iota(jnp.int32, (rows, STEP), 0) < slots_ref[len(sizes)]
        mixed = jnp.where(live, total[:rows, :] * (1.0 / MOMENT_SCALE), 0.0)
        mixed_ref[...] = mixed

        @pl.when(pl.program_id(0) == 0)
        def _():
            projected_ref[...] = jnp.zeros((rows, RANK), jnp.float32)

        projected_ref[...] += split_product(split(mixed), split(basis_ref[...]))

    grid_spec = pltpu.PrefetchScalarGridSpec(
        num_scalar_prefetch=1,
        grid=(cols // STEP,),
        in_specs=[pl.BlockSpec((size, STEP), lambda t, *_: (0, t)) for size in sizes]
        + [
            pl.BlockSpec((cap, STEP), lambda t, *_: (0, t)),
            pl.BlockSpec((STEP, RANK), lambda t, *_: (t, 0)),
        ],
        out_specs=[
            pl.BlockSpec((rows, STEP), lambda t, *_: (0, t)),
            pl.BlockSpec((rows, RANK), lambda t, *_: (0, 0)),
        ],
        scratch_shapes=[pltpu.VMEM((top, STEP), jnp.float32)],
    )
    return pl.pallas_call(
        kernel,
        grid_spec=grid_spec,
        out_shape=[
            jax.ShapeDtypeStruct((rows, cols), jnp.float32),
            jax.ShapeDtypeStruct((rows, RANK), jnp.float32),
        ],
        compiler_params=pltpu.CompilerParams(vmem_limit_bytes=VMEM_LIMIT),
    )(slots, *landed, grad_rows, basis)


def dot(a, b, dims):
    return lax.dot_general(a, b, dims, precision=HIGHEST, preferred_element_type=jnp.float32)


def invert_factor(left, right, out_ref):
    size = left.shape[0]
    contract = (((1,), (1,)), ((), ()))
    rows = lax.broadcasted_iota(jnp.int32, (size, size), 0)
    cols = lax.broadcasted_iota(jnp.int32, (size, size), 1)
    right[...] = jnp.where(rows == cols, 1.0, 0.0)
    row = lax.broadcasted_iota(jnp.int32, (PANEL, PANEL), 0)
    col = lax.broadcasted_iota(jnp.int32, (PANEL, PANEL), 1)
    for start in range(0, size, PANEL):
        stop = start + PANEL
        block = left[start:stop, start:stop]
        unit = jnp.where(row == col, 1.0, 0.0)
        pivots = jnp.ones((PANEL, PANEL), jnp.float32)
        for first in range(0, PANEL, GROUP):
            heads = [
                jnp.broadcast_to(block[:, k : k + 1], (PANEL, PANEL))
                for k in range(first, first + GROUP)
            ]
            for k in range(first, first + GROUP):
                head = heads[k - first]
                pivot = head[k : k + 1, :]
                ratio = jnp.where(row > k, head * (1.0 / pivot), 0.0)
                pivots = jnp.where(row == k, pivot, pivots)
                for later in range(k + 1, first + GROUP):
                    other = heads[later - first]
                    heads[later - first] = other - ratio * other[k : k + 1, :]
                if first + GROUP < PANEL:
                    block = block - ratio * block[k : k + 1, :]
                unit = unit - ratio * unit[k : k + 1, :]
        inverse = unit * lax.rsqrt(pivots)
        strip = dot(inverse, right[start:stop, :], (((1,), (0,)), ((), ())))
        out_ref[start:stop, :] = strip
        if stop < size:
            lower = dot(left[stop:, start:stop], inverse, contract)
            left[stop:, stop:] -= dot(lower, lower, contract)
            right[stop:, :] -= dot(lower, strip, (((1,), (0,)), ((), ())))


def finish(slots, mine, other, basis, projected, mixed, landed, sizes, cap):
    half, cols = mine.shape
    rows = mixed.shape[0]
    tiles = cols // STEP
    top = -(-cap // TILE) * TILE + max(sizes)
    plain = (((1,), (0,)), ((), ()))
    contract = (((1,), (1,)), ((), ()))

    def kernel(slots_ref, mine_ref, other_ref, basis_ref, projected_ref, mixed_ref, *refs):
        values = refs[: len(sizes)]
        weight_ref, moment_ref, scaled_ref = refs[len(sizes) : len(sizes) + 3]
        held, total, left, right, inverse, rms_ref, high, low = refs[len(sizes) + 3 :]
        step = pl.program_id(0)

        @pl.when(step == 0)
        def _():
            left[...] = jnp.zeros((RANK, RANK), jnp.float32)
            rms_ref[...] = jnp.zeros((RANK, 128), jnp.float32)

        @pl.when(step < tiles)
        def _():
            lower = slots_ref[len(sizes) + 1] == 0
            held[step, :half] = jnp.where(lower, mine_ref[...], other_ref[...])
            held[step, half:] = jnp.where(lower, other_ref[...], mine_ref[...])
            left[...] += dot(held[step], basis_ref[...], plain)

        @pl.when(step == tiles - 1)
        def _():
            invert_factor(left, right, inverse)

        @pl.when((step >= tiles) & (step < 2 * tiles))
        def _():
            reduced = split_product(split(inverse[...]), split(held[step - tiles]))
            held[step - tiles] = reduced
            rms_ref[...] += jnp.broadcast_to(
                jnp.sum(reduced * reduced, axis=1, keepdims=True), (RANK, 128)
            )

        @pl.when(step == 2 * tiles - 1)
        def _():
            rms = jnp.sqrt(rms_ref[...] * (1.0 / cols) + epsilon)
            rms_ref[...] = rms
            rate = learn_rate * update_rms * math.sqrt(HIDDEN_ROWS / RANK)
            for_moment = dot(projected_ref[...], (1.0 - momentum_rate) * inverse[...], contract)
            for_weight = dot(projected_ref[...], inverse[...] * (rate / rms[:, :1]), contract)
            high[:rows, :], low[:rows, :] = split(for_moment)
            high[rows:, :], low[rows:, :] = split(for_weight)

        @pl.when(step >= 2 * tiles)
        def _():
            total[...] = jnp.zeros((top, STEP), jnp.float32)
            place_rounds(total, values, slots_ref, sizes)
            reduced = held[step - 2 * tiles]
            scaled_ref[...] = (reduced / rms_ref[:, :1]).T
            change = split_product((high[...], low[...]), split(reduced))
            live = lax.broadcasted_iota(jnp.int32, (cap, STEP), 0) < slots_ref[len(sizes)]
            kept = total[:cap, :] * ((1.0 - learn_rate * decay_rate) / WEIGHT_SCALE)
            weight_ref[...] = jnp.where(live, kept - change[rows : rows + cap], 0.0)
            moment_ref[...] = mixed_ref[:cap, :] - change[:cap]

    def first(t, *_):
        return jnp.minimum(t, tiles - 1)

    def third(t, *_):
        return jnp.maximum(t - 2 * tiles, 0)

    square = pltpu.VMEM((RANK, RANK), jnp.float32)
    grid_spec = pltpu.PrefetchScalarGridSpec(
        num_scalar_prefetch=1,
        grid=(3 * tiles,),
        in_specs=[
            pl.BlockSpec((half, STEP), lambda t, *_: (0, first(t))),
            pl.BlockSpec((half, STEP), lambda t, *_: (0, first(t))),
            pl.BlockSpec((STEP, RANK), lambda t, *_: (first(t), 0)),
            pl.BlockSpec((rows, RANK), lambda t, *_: (0, 0)),
            pl.BlockSpec((rows, STEP), lambda t, *_: (0, third(t))),
        ]
        + [pl.BlockSpec((size, STEP), lambda t, *_: (0, third(t))) for size in sizes],
        out_specs=[
            pl.BlockSpec((cap, STEP), lambda t, *_: (0, third(t))),
            pl.BlockSpec((cap, STEP), lambda t, *_: (0, third(t))),
            pl.BlockSpec((STEP, RANK), lambda t, *_: (third(t), 0)),
        ],
        scratch_shapes=[
            pltpu.VMEM((tiles, RANK, STEP), jnp.float32),
            pltpu.VMEM((top, STEP), jnp.float32),
            square,
            square,
            square,
            pltpu.VMEM((RANK, 128), jnp.float32),
            pltpu.VMEM((2 * rows, RANK), jnp.bfloat16),
            pltpu.VMEM((2 * rows, RANK), jnp.bfloat16),
        ],
    )
    return pl.pallas_call(
        kernel,
        grid_spec=grid_spec,
        out_shape=[
            jax.ShapeDtypeStruct((cap, cols), jnp.float32),
            jax.ShapeDtypeStruct((cap, cols), jnp.float32),
            jax.ShapeDtypeStruct((cols, RANK), jnp.float32),
        ],
        compiler_params=pltpu.CompilerParams(vmem_limit_bytes=FINISH_LIMIT),
    )(slots, mine, other, basis, projected, mixed, *landed)


def flip(value, count, bit):
    return lax.ppermute(value, AXES, [(i, i ^ (1 << bit)) for i in range(count)])


def after(value, stage):
    if stage is None:
        return value
    first = stage.reshape(-1)[0].astype(jnp.float32)
    return value + jnp.minimum(jnp.abs(first), 0.0)


def gather_bits(value, held, me, count, order):
    held = list(held)
    for bit in order:
        other = flip(value, count, bit)
        axis = sum(b > bit for b in held)
        mine = (me >> bit) & 1
        value = jnp.where(
            mine == 0, jnp.stack([value, other], axis), jnp.stack([other, value], axis)
        )
        held.append(bit)
    return value


def scatter_bits(value, held, me, count, order):
    held = sorted(held, reverse=True)
    for bit in order:
        axis = held.index(bit)
        mine = (me >> bit) & 1
        send = lax.dynamic_index_in_dim(value, 1 - mine, axis, keepdims=False)
        keep = lax.dynamic_index_in_dim(value, mine, axis, keepdims=False)
        value = keep + flip(send, count, bit)
        held.remove(bit)
    return value


def sum_chips(value, me, count):
    bits = count.bit_length() - 1
    rows, cols = value.shape
    half = cols // 2
    links, rest = list(range(1, bits)), list(range(3, bits))
    cube = value.reshape((2,) * (bits - 1) + (2 * rows // count, cols))
    near = scatter_bits(cube[..., :half], links, me, count, [1, 2])
    far = scatter_bits(cube[..., half:], links, me, count, [2, 1])
    cube = jnp.concatenate([near, far], axis=-1)
    cube = scatter_bits(cube, rest, me, count, rest[:-1])
    cube = cube + flip(cube, count, rest[-1])
    return gather_chips(cube, rest[-1:], me, count).reshape(rows, cols)


def gather_chips(block, held, me, count, stage=None):
    bits = count.bit_length() - 1
    half = block.shape[-1] // 2
    rest = list(range(3, bits))
    cube = gather_bits(block, held, me, count, [bit for bit in rest[::-1] if bit not in held])
    near = gather_bits(cube[..., :half], rest, me, count, [2])
    far = gather_bits(cube[..., half:], rest, me, count, [1])
    near = gather_bits(after(near, stage), rest + [2], me, count, [1])
    far = gather_bits(after(far, stage), rest + [1], me, count, [2])
    return jnp.concatenate([near, far], axis=-1)


def on_device(weight_rows, moment_rows, grad_rows, basis, old_bounds, new_bounds):
    hosts, per_host = lax.axis_size("hst"), lax.axis_size("dev")
    count = hosts * per_host
    old_cap, cols = weight_rows.shape
    new_cap = grad_rows.shape[0]
    me = lax.axis_index("hst") * per_host + lax.axis_index("dev")

    ranges = [new_ranges(lost, hosts, per_host) for lost in range(1, hosts - 1)]
    sizes = SIZES
    plans = [plan_chain(bounds, old_cap, sizes, per_host) for bounds in ranges]
    if any(rounds is None for rounds in plans):
        sizes = (-(-old_cap // 16) * 16,)
        plans = [plan_greedy(bounds, old_cap, sizes) for bounds in ranges]
        sizes = sizes * max(len(rounds) for rounds in plans)
    number = len(sizes)
    plans = [rounds + [[]] * (number - len(rounds)) for rounds in plans]
    first_rows = np.zeros((hosts - 2, count, number), np.int32)
    slot_tiles = np.zeros((hosts - 2, count, number), np.int32)
    for index, rounds in enumerate(plans):
        bounds = new_ranges(index + 1, hosts, per_host)
        for k, held in enumerate(rounds):
            for src, dst, slot in held:
                first_rows[index, src, k] = bounds[dst] + slot
                slot_tiles[index, dst, k] = slot // TILE

    bits = count.bit_length() - 1
    place = jnp.full((1,), me, jnp.int32)
    packed = pack_rows(
        weight_rows,
        moment_rows,
        jnp.asarray(first_rows.reshape(-1)),
        place,
        old_bounds,
        new_bounds,
        sizes,
        hosts,
    )
    full_basis = gather_chips(basis, [], me, count, packed[0])
    full_basis = gather_bits(full_basis, range(1, bits), me, count, [0]).reshape(cols, RANK)

    edges = new_bounds[::per_host]
    lost = jnp.argmax(edges[1:] == edges[:-1]).astype(jnp.int32)
    case = jnp.clip(lost - 1, 0, hosts - 3)

    def send(rounds):
        def branch(*values):
            landed = [
                lax.ppermute(value.astype(WIRE), AXES, [(src, dst) for src, dst, _ in held])
                for value, held in zip(values, rounds)
            ]
            moments = [value[:, :cols].astype(jnp.float32) for value in landed]
            weights = [value[:, cols:].astype(jnp.float32) for value in landed]
            return (*moments, *weights)

        return branch

    case = case + after(jnp.zeros((), jnp.float32), full_basis).astype(jnp.int32)
    landed = lax.switch(case, [send(rounds) for rounds in plans], *packed)
    moments, weights = landed[:number], landed[number:]
    line = lax.dynamic_slice(jnp.asarray(slot_tiles), (case, me, 0), (1, 1, number))[0, 0]
    new_range = lax.dynamic_slice_in_dim(new_bounds, me, 2)
    slots = jnp.concatenate([line, new_range[1:] - new_range[:1], jnp.full((1,), me & 1, jnp.int32)])

    mixed, projected = mix_and_project(moments, slots, grad_rows, full_basis, sizes)

    def part(number):
        factor_part = lax.dynamic_slice_in_dim(projected, number * (RANK // 2), RANK // 2, 1)
        return jnp.dot(factor_part.T, mixed, precision=HIGH)

    away = flip(part(1 - (me & 1)), count, 0)
    kept = lax.optimization_barrier(part(me & 1))
    mine = sum_chips(kept + away, me, count)
    other = flip(mine, count, 0)
    return tuple(
        finish(slots, mine, other, full_basis, projected, mixed, weights, sizes, new_cap)
    )


def solution(mesh):
    return jax.shard_map(
        on_device,
        mesh=mesh,
        in_specs=(P(AXES, None), P(AXES, None), P(AXES, None), P(AXES, None), P(), P()),
        out_specs=(P(AXES, None), P(AXES, None), P()),
        check_vma=False,
    )
```

```python
import math

import jax
import jax.numpy as jnp
import numpy as np
from jax import lax
from jax.experimental import pallas as pl
from jax.experimental.pallas import tpu as pltpu
from jax.sharding import PartitionSpec as P

HIDDEN_ROWS = 8192
RANK = 256
AXES = ("hst", "dev")
HIGHEST = lax.Precision.HIGHEST
HIGH = lax.Precision.HIGH

momentum_rate = 0.6
learn_rate = 0.1
decay_rate = 0.5
update_rms = 0.2
epsilon = 1e-06

TILE = 8
SIZES = (144, 96, 80, 64, 48)
STEP = 768
PANEL = 64
GROUP = 16
VMEM_LIMIT = 16 * 2**20
FINISH_LIMIT = 60 * 2**20
WIRE = jnp.float16
WEIGHT_SCALE = 2.0**15
MOMENT_SCALE = 2.0**13


def new_ranges(lost, hosts, per_host):
    left = (hosts - 1) * per_host
    ids = np.arange(hosts * per_host + 1)
    first = lost * per_host
    rank = np.where(ids <= first, ids, np.maximum(ids - per_host, first))
    return rank * HIDDEN_ROWS // left


def row_windows(bounds, old_cap):
    count = len(bounds) - 1
    even = HIDDEN_ROWS // count
    windows = []
    for dst in range(count):
        for src in range(count):
            low = max(bounds[dst], src * even) - bounds[dst]
            high = min(bounds[dst + 1], src * even + old_cap, HIDDEN_ROWS) - bounds[dst]
            if low < high:
                windows.append((dst, src, int(low) // TILE * TILE, int(high)))
    return windows


def plan_greedy(bounds, old_cap, sizes):
    rounds = []
    for dst, src, low, high in row_windows(bounds, old_cap):
        while low < high:
            for held in rounds:
                if all(src != a and dst != b for a, b, _ in held):
                    break
            else:
                held = []
                rounds.append(held)
            held.append((src, dst, low))
            low += sizes[0]
    return rounds


def plan_chain(bounds, old_cap, sizes, per_host):
    windows = row_windows(bounds, old_cap)
    number = len(sizes)
    totals = [sum(sizes[k] for k in range(number) if m >> k & 1) for m in range(1 << number)]
    states, trail = {(0, 0): (0.0, None, 0)}, []
    last_dst = last_src = None
    for dst, src, low, high in windows:
        need = high - low
        sets = [
            m
            for m in range(1, 1 << number)
            if totals[m] >= need
            and all(totals[m] - sizes[k] < need for k in range(number) if m >> k & 1)
        ]
        weight = 0.01 + (src // per_host != dst // per_host)
        following = {}
        for state, (cost, _, _) in states.items():
            at_dst = state[0] if dst == last_dst else 0
            at_src = state[1] if src == last_src else 0
            for m in sets:
                if m & (at_dst | at_src):
                    continue
                key, price = (at_dst | m, at_src | m), cost + weight * totals[m]
                if key not in following or price < following[key][0]:
                    following[key] = (price, state, m)
        if not following:
            return None
        trail.append(following)
        states, last_dst, last_src = following, dst, src
    state = min(states, key=lambda key: (states[key][0], key))
    rounds = [[] for _ in sizes]
    for (dst, src, low, _), following in zip(windows[::-1], trail[::-1]):
        _, previous, m = following[state]
        for k in range(number):
            if m >> k & 1:
                rounds[k].append((src, dst, low))
                low += sizes[k]
        state = previous
    for held in rounds:
        if len({a for a, _, _ in held}) < len(held) or len({b for _, b, _ in held}) < len(held):
            return None
    return rounds


def pack_rows(weight_rows, moment_rows, table, place, old_bounds, new_bounds, sizes, hosts):
    cap, cols = weight_rows.shape
    tiles = cols // STEP
    number = len(sizes)
    widest = max(sizes)
    count = old_bounds.shape[0] - 1
    per_host = count // hosts

    def kernel(table_ref, place_ref, old_ref, new_ref, weight_ref, moment_ref, *rest):
        outs, (held, starts) = rest[:-2], rest[-2:]
        tile = pl.program_id(0)

        @pl.when(tile == 0)
        def _():
            me = place_ref[0]
            case = jnp.int32(0)
            for host in range(1, hosts - 1):
                empty = new_ref[host * per_host] == new_ref[(host + 1) * per_host]
                case = jnp.where(empty, host - 1, case)
            first = old_ref[me]
            starts[number] = old_ref[me + 1] - first
            for index in range(number):
                row = table_ref[(case * count + me) * number + index] - first
                starts[index] = jnp.clip(row, -widest, cap) + widest
            held[:widest, :] = jnp.zeros((widest, STEP), jnp.float32)
            held[widest + cap :, :] = jnp.zeros((held.shape[0] - widest - cap, STEP), jnp.float32)

        own = lax.broadcasted_iota(jnp.int32, (cap, STEP), 0) < starts[number]

        @pl.when(tile < tiles)
        def _():
            held[widest : widest + cap, :] = jnp.where(own, moment_ref[...] * MOMENT_SCALE, 0.0)

        @pl.when(tile >= tiles)
        def _():
            held[widest : widest + cap, :] = jnp.where(own, weight_ref[...] * WEIGHT_SCALE, 0.0)

        for index, size in enumerate(sizes):
            start = starts[index]
            base = pl.multiple_of(start // 8 * 8, 8)
            window = held[pl.ds(base, size + 8), :]
            shift = lax.rem(size + 8 - (start - base), size + 8)
            outs[index][...] = pltpu.roll(window, shift, 0)[:size]

    grid_spec = pltpu.PrefetchScalarGridSpec(
        num_scalar_prefetch=4,
        grid=(2 * tiles,),
        in_specs=[
            pl.BlockSpec((cap, STEP), lambda t, *_: (0, jnp.maximum(t - tiles, 0))),
            pl.BlockSpec((cap, STEP), lambda t, *_: (0, jnp.minimum(t, tiles - 1))),
        ],
        out_specs=[pl.BlockSpec((size, STEP), lambda t, *_: (0, t)) for size in sizes],
        scratch_shapes=[
            pltpu.VMEM((cap + 2 * widest + 8, STEP), jnp.float32),
            pltpu.SMEM((number + 1,), jnp.int32),
        ],
    )
    return pl.pallas_call(
        kernel,
        grid_spec=grid_spec,
        out_shape=[jax.ShapeDtypeStruct((size, 2 * cols), jnp.float32) for size in sizes],
        cost_estimate=pl.CostEstimate(
            flops=0, bytes_accessed=int(8 * (cap + sum(sizes)) * cols), transcendentals=0
        ),
        compiler_params=pltpu.CompilerParams(vmem_limit_bytes=VMEM_LIMIT),
    )(table, place, old_bounds, new_bounds, weight_rows, moment_rows)


def split(value):
    high = value.astype(jnp.bfloat16)
    return high, (value - high.astype(jnp.float32)).astype(jnp.bfloat16)


def split_product(left, right):
    def dot(a, b):
        return jnp.dot(a, b, preferred_element_type=jnp.float32)

    return dot(left[0], right[0]) + (dot(left[0], right[1]) + dot(left[1], right[0]))


def place_rounds(total, values, slots_ref, sizes):
    for index, size in enumerate(sizes):
        at = pl.multiple_of(slots_ref[index] * TILE, TILE)
        total[pl.ds(at, size), :] += values[index][...]


def mix_and_project(landed, slots, grad_rows, basis, sizes):
    cap, cols = grad_rows.shape
    rows = -(-cap // 8) * 8
    top = -(-cap // TILE) * TILE + max(sizes)

    def kernel(slots_ref, *refs):
        values, (grad_ref, basis_ref, mixed_ref, projected_ref, total) = refs[: len(sizes)], refs[len(sizes) :]
        total[...] = jnp.zeros((top, STEP), jnp.float32)
        total[:cap, :] = grad_ref[...].astype(jnp.float32) * MOMENT_SCALE
        place_rounds(total, values, slots_ref, sizes)
        live = lax.broadcasted_iota(jnp.int32, (rows, STEP), 0) < slots_ref[len(sizes)]
        mixed = jnp.where(live, total[:rows, :] * (1.0 / MOMENT_SCALE), 0.0)
        mixed_ref[...] = mixed

        @pl.when(pl.program_id(0) == 0)
        def _():
            projected_ref[...] = jnp.zeros((rows, RANK), jnp.float32)

        projected_ref[...] += split_product(split(mixed), split(basis_ref[...]))

    grid_spec = pltpu.PrefetchScalarGridSpec(
        num_scalar_prefetch=1,
        grid=(cols // STEP,),
        in_specs=[pl.BlockSpec((size, STEP), lambda t, *_: (0, t)) for size in sizes]
        + [
            pl.BlockSpec((cap, STEP), lambda t, *_: (0, t)),
            pl.BlockSpec((STEP, RANK), lambda t, *_: (t, 0)),
        ],
        out_specs=[
            pl.BlockSpec((rows, STEP), lambda t, *_: (0, t)),
            pl.BlockSpec((rows, RANK), lambda t, *_: (0, 0)),
        ],
        scratch_shapes=[pltpu.VMEM((top, STEP), jnp.float32)],
    )
    return pl.pallas_call(
        kernel,
        grid_spec=grid_spec,
        out_shape=[
            jax.ShapeDtypeStruct((rows, cols), jnp.float32),
            jax.ShapeDtypeStruct((rows, RANK), jnp.float32),
        ],
        compiler_params=pltpu.CompilerParams(vmem_limit_bytes=VMEM_LIMIT),
    )(slots, *landed, grad_rows, basis)


def dot(a, b, dims):
    return lax.dot_general(a, b, dims, precision=HIGHEST, preferred_element_type=jnp.float32)


def invert_factor(left, right, out_ref):
    size = left.shape[0]
    contract = (((1,), (1,)), ((), ()))
    rows = lax.broadcasted_iota(jnp.int32, (size, size), 0)
    cols = lax.broadcasted_iota(jnp.int32, (size, size), 1)
    right[...] = jnp.where(rows == cols, 1.0, 0.0)
    row = lax.broadcasted_iota(jnp.int32, (PANEL, PANEL), 0)
    col = lax.broadcasted_iota(jnp.int32, (PANEL, PANEL), 1)
    for start in range(0, size, PANEL):
        stop = start + PANEL
        block = left[start:stop, start:stop]
        unit = jnp.where(row == col, 1.0, 0.0)
        pivots = jnp.ones((PANEL, PANEL), jnp.float32)
        for first in range(0, PANEL, GROUP):
            heads = [
                jnp.broadcast_to(block[:, k : k + 1], (PANEL, PANEL))
                for k in range(first, first + GROUP)
            ]
            for k in range(first, first + GROUP):
                head = heads[k - first]
                pivot = head[k : k + 1, :]
                ratio = jnp.where(row > k, head * (1.0 / pivot), 0.0)
                pivots = jnp.where(row == k, pivot, pivots)
                for later in range(k + 1, first + GROUP):
                    other = heads[later - first]
                    heads[later - first] = other - ratio * other[k : k + 1, :]
                if first + GROUP < PANEL:
                    block = block - ratio * block[k : k + 1, :]
                unit = unit - ratio * unit[k : k + 1, :]
        inverse = unit * lax.rsqrt(pivots)
        strip = dot(inverse, right[start:stop, :], (((1,), (0,)), ((), ())))
        out_ref[start:stop, :] = strip
        if stop < size:
            lower = dot(left[stop:, start:stop], inverse, contract)
            left[stop:, stop:] -= dot(lower, lower, contract)
            right[stop:, :] -= dot(lower, strip, (((1,), (0,)), ((), ())))


def finish(slots, mine, other, basis, projected, mixed, landed, sizes, cap):
    half, cols = mine.shape
    rows = mixed.shape[0]
    tiles = cols // STEP
    top = -(-cap // TILE) * TILE + max(sizes)
    plain = (((1,), (0,)), ((), ()))
    contract = (((1,), (1,)), ((), ()))

    def kernel(slots_ref, mine_ref, other_ref, basis_ref, projected_ref, mixed_ref, *refs):
        values = refs[: len(sizes)]
        weight_ref, moment_ref, scaled_ref = refs[len(sizes) : len(sizes) + 3]
        held, total, left, right, inverse, rms_ref, high, low = refs[len(sizes) + 3 :]
        step = pl.program_id(0)

        @pl.when(step == 0)
        def _():
            left[...] = jnp.zeros((RANK, RANK), jnp.float32)
            rms_ref[...] = jnp.zeros((RANK, 128), jnp.float32)

        @pl.when(step < tiles)
        def _():
            lower = slots_ref[len(sizes) + 1] == 0
            held[step, :half] = jnp.where(lower, mine_ref[...], other_ref[...])
            held[step, half:] = jnp.where(lower, other_ref[...], mine_ref[...])
            left[...] += dot(held[step], basis_ref[...], plain)

        @pl.when(step == tiles - 1)
        def _():
            invert_factor(left, right, inverse)

        @pl.when((step >= tiles) & (step < 2 * tiles))
        def _():
            reduced = split_product(split(inverse[...]), split(held[step - tiles]))
            held[step - tiles] = reduced
            rms_ref[...] += jnp.broadcast_to(
                jnp.sum(reduced * reduced, axis=1, keepdims=True), (RANK, 128)
            )

        @pl.when(step == 2 * tiles - 1)
        def _():
            rms = jnp.sqrt(rms_ref[...] * (1.0 / cols) + epsilon)
            rms_ref[...] = rms
            rate = learn_rate * update_rms * math.sqrt(HIDDEN_ROWS / RANK)
            for_moment = dot(projected_ref[...], (1.0 - momentum_rate) * inverse[...], contract)
            for_weight = dot(projected_ref[...], inverse[...] * (rate / rms[:, :1]), contract)
            high[:rows, :], low[:rows, :] = split(for_moment)
            high[rows:, :], low[rows:, :] = split(for_weight)

        @pl.when(step >= 2 * tiles)
        def _():
            total[...] = jnp.zeros((top, STEP), jnp.float32)
            place_rounds(total, values, slots_ref, sizes)
            reduced = held[step - 2 * tiles]
            scaled_ref[...] = (reduced / rms_ref[:, :1]).T
            change = split_product((high[...], low[...]), split(reduced))
            live = lax.broadcasted_iota(jnp.int32, (cap, STEP), 0) < slots_ref[len(sizes)]
            kept = total[:cap, :] * ((1.0 - learn_rate * decay_rate) / WEIGHT_SCALE)
            weight_ref[...] = jnp.where(live, kept - change[rows : rows + cap], 0.0)
            moment_ref[...] = mixed_ref[:cap, :] - change[:cap]

    def first(t, *_):
        return jnp.minimum(t, tiles - 1)

    def third(t, *_):
        return jnp.maximum(t - 2 * tiles, 0)

    square = pltpu.VMEM((RANK, RANK), jnp.float32)
    grid_spec = pltpu.PrefetchScalarGridSpec(
        num_scalar_prefetch=1,
        grid=(3 * tiles,),
        in_specs=[
            pl.BlockSpec((half, STEP), lambda t, *_: (0, first(t))),
            pl.BlockSpec((half, STEP), lambda t, *_: (0, first(t))),
            pl.BlockSpec((STEP, RANK), lambda t, *_: (first(t), 0)),
            pl.BlockSpec((rows, RANK), lambda t, *_: (0, 0)),
            pl.BlockSpec((rows, STEP), lambda t, *_: (0, third(t))),
        ]
        + [pl.BlockSpec((size, STEP), lambda t, *_: (0, third(t))) for size in sizes],
        out_specs=[
            pl.BlockSpec((cap, STEP), lambda t, *_: (0, third(t))),
            pl.BlockSpec((cap, STEP), lambda t, *_: (0, third(t))),
            pl.BlockSpec((STEP, RANK), lambda t, *_: (third(t), 0)),
        ],
        scratch_shapes=[
            pltpu.VMEM((tiles, RANK, STEP), jnp.float32),
            pltpu.VMEM((top, STEP), jnp.float32),
            square,
            square,
            square,
            pltpu.VMEM((RANK, 128), jnp.float32),
            pltpu.VMEM((2 * rows, RANK), jnp.bfloat16),
            pltpu.VMEM((2 * rows, RANK), jnp.bfloat16),
        ],
    )
    return pl.pallas_call(
        kernel,
        grid_spec=grid_spec,
        out_shape=[
            jax.ShapeDtypeStruct((cap, cols), jnp.float32),
            jax.ShapeDtypeStruct((cap, cols), jnp.float32),
            jax.ShapeDtypeStruct((cols, RANK), jnp.float32),
        ],
        compiler_params=pltpu.CompilerParams(vmem_limit_bytes=FINISH_LIMIT),
    )(slots, mine, other, basis, projected, mixed, *landed)


def flip(value, count, bit):
    return lax.ppermute(value, AXES, [(i, i ^ (1 << bit)) for i in range(count)])


def after(value, stage):
    if stage is None:
        return value
    first = stage.reshape(-1)[0].astype(jnp.float32)
    return value + jnp.minimum(jnp.abs(first), 0.0)


def gather_bits(value, held, me, count, order):
    held = list(held)
    for bit in order:
        other = flip(value, count, bit)
        axis = sum(b > bit for b in held)
        mine = (me >> bit) & 1
        value = jnp.where(
            mine == 0, jnp.stack([value, other], axis), jnp.stack([other, value], axis)
        )
        held.append(bit)
    return value


def scatter_bits(value, held, me, count, order):
    held = sorted(held, reverse=True)
    for bit in order:
        axis = held.index(bit)
        mine = (me >> bit) & 1
        send = lax.dynamic_index_in_dim(value, 1 - mine, axis, keepdims=False)
        keep = lax.dynamic_index_in_dim(value, mine, axis, keepdims=False)
        value = keep + flip(send, count, bit)
        held.remove(bit)
    return value


def sum_chips(value, me, count):
    bits = count.bit_length() - 1
    rows, cols = value.shape
    half = cols // 2
    links, rest = list(range(1, bits)), list(range(3, bits))
    cube = value.reshape((2,) * (bits - 1) + (2 * rows // count, cols))
    near = scatter_bits(cube[..., :half], links, me, count, [1, 2])
    far = scatter_bits(cube[..., half:], links, me, count, [2, 1])
    cube = jnp.concatenate([near, far], axis=-1)
    cube = scatter_bits(cube, rest, me, count, rest[:-1])
    cube = cube + flip(cube, count, rest[-1])
    return gather_chips(cube, rest[-1:], me, count).reshape(rows, cols)


def gather_chips(block, held, me, count, stage=None):
    bits = count.bit_length() - 1
    half = block.shape[-1] // 2
    rest = list(range(3, bits))
    cube = gather_bits(block, held, me, count, [bit for bit in rest[::-1] if bit not in held])
    near = gather_bits(cube[..., :half], rest, me, count, [2])
    far = gather_bits(cube[..., half:], rest, me, count, [1])
    near = gather_bits(after(near, stage), rest + [2], me, count, [1])
    far = gather_bits(after(far, stage), rest + [1], me, count, [2])
    return jnp.concatenate([near, far], axis=-1)


def on_device(weight_rows, moment_rows, grad_rows, basis, old_bounds, new_bounds):
    hosts, per_host = lax.axis_size("hst"), lax.axis_size("dev")
    count = hosts * per_host
    old_cap, cols = weight_rows.shape
    new_cap = grad_rows.shape[0]
    me = lax.axis_index("hst") * per_host + lax.axis_index("dev")

    ranges = [new_ranges(lost, hosts, per_host) for lost in range(1, hosts - 1)]
    sizes = SIZES
    plans = [plan_chain(bounds, old_cap, sizes, per_host) for bounds in ranges]
    if any(rounds is None for rounds in plans):
        sizes = (-(-old_cap // 16) * 16,)
        plans = [plan_greedy(bounds, old_cap, sizes) for bounds in ranges]
        sizes = sizes * max(len(rounds) for rounds in plans)
    number = len(sizes)
    plans = [rounds + [[]] * (number - len(rounds)) for rounds in plans]
    first_rows = np.zeros((hosts - 2, count, number), np.int32)
    slot_tiles = np.zeros((hosts - 2, count, number), np.int32)
    for index, rounds in enumerate(plans):
        bounds = new_ranges(index + 1, hosts, per_host)
        for k, held in enumerate(rounds):
            for src, dst, slot in held:
                first_rows[index, src, k] = bounds[dst] + slot
                slot_tiles[index, dst, k] = slot // TILE

    bits = count.bit_length() - 1
    place = jnp.full((1,), me, jnp.int32)
    packed = pack_rows(
        weight_rows,
        moment_rows,
        jnp.asarray(first_rows.reshape(-1)),
        place,
        old_bounds,
        new_bounds,
        sizes,
        hosts,
    )
    full_basis = gather_chips(basis, [], me, count, packed[0])
    full_basis = gather_bits(full_basis, range(1, bits), me, count, [0]).reshape(cols, RANK)

    edges = new_bounds[::per_host]
    lost = jnp.argmax(edges[1:] == edges[:-1]).astype(jnp.int32)
    case = jnp.clip(lost - 1, 0, hosts - 3)

    def send(rounds):
        def branch(*values):
            landed = [
                lax.ppermute(value.astype(WIRE), AXES, [(src, dst) for src, dst, _ in held])
                for value, held in zip(values, rounds)
            ]
            moments = [value[:, :cols].astype(jnp.float32) for value in landed]
            weights = [value[:, cols:].astype(jnp.float32) for value in landed]
            return (*moments, *weights)

        return branch

    case = case + after(jnp.zeros((), jnp.float32), full_basis).astype(jnp.int32)
    landed = lax.switch(case, [send(rounds) for rounds in plans], *packed)
    moments, weights = landed[:number], landed[number:]
    line = lax.dynamic_slice(jnp.asarray(slot_tiles), (case, me, 0), (1, 1, number))[0, 0]
    new_range = lax.dynamic_slice_in_dim(new_bounds, me, 2)
    slots = jnp.concatenate([line, new_range[1:] - new_range[:1], jnp.full((1,), me & 1, jnp.int32)])

    mixed, projected = mix_and_project(moments, slots, grad_rows, full_basis, sizes)

    def part(number):
        factor_part = lax.dynamic_slice_in_dim(projected, number * (RANK // 2), RANK // 2, 1)
        return jnp.dot(factor_part.T, mixed, precision=HIGH)

    away = flip(part(1 - (me & 1)), count, 0)
    kept = lax.optimization_barrier(part(me & 1))
    mine = sum_chips(kept + away, me, count)
    other = flip(mine, count, 0)
    return tuple(
        finish(slots, mine, other, full_basis, projected, mixed, weights, sizes, new_cap)
    )


def solution(mesh):
    return jax.shard_map(
        on_device,
        mesh=mesh,
        in_specs=(P(AXES, None), P(AXES, None), P(AXES, None), P(AXES, None), P(), P()),
        out_specs=(P(AXES, None), P(AXES, None), P()),
        check_vma=False,
    )
```
